256 devices in a mesh: ctx: 64 (over z, y, core), tp: 4 (over x).
Axes of the slice: x: 4, y: 4, z: 8, core: 2. Of those that a mesh axis runs over, the one named last changes fastest.
Arguments:
- tokens: bfloat16 [32768, 5376], P(('ctx', 'tp')), may hold values from -8 to 8
- positions: int32 [32768], replicated, may hold values from 0 to 131071, as said below
- w_query: bfloat16 [5376, 2048], P('ctx', 'tp'), may hold values from -1 to 1
- key_matrix: bfloat16 [5376, 1024], P('ctx', 'tp'), may hold values from -1 to 1
- value_matrix: bfloat16 [5376, 1024], P('ctx', 'tp'), may hold values from -0.078125 to 0.078125
- w_out: bfloat16 [2048, 5376], P('tp', 'ctx'), may hold values from -0.125 to 0.125
- gain_in: float32 [5376], replicated, may hold values from 0.1 to 1.9
- gain_query: float32 [128], replicated, may hold values from 0.5 to 14
- gain_key: float32 [128], replicated, may hold values from 0.5 to 14
- gain_post: float32 [5376], replicated, may hold values from 0.1 to 1.9
Outputs:
- layer_out: bfloat16 [32768, 5376], P(('ctx', 'tp'))
The draws below stay inside these ranges and needn't reach their ends.
Inputs may be any that keep to these rules, and one draw needn't show every extreme that they name: (positions) rise strictly along the tokens, by 1 to 4 from one token to the next, and the last token stands at 131071.
All inputs are finite; a program needn't handle non-finite values.
Results may differ from the reference program's by a relative error of at most 0.013.
The reference program's roundings to bfloat16 on the way count: a program that leaves them out, or rounds other values in their place, can miss the bound.
Values may be sent and summed in bfloat16 or wider, within the bound.
No kernel may reach another device: no remote copies, remote signals or barrier semaphores. Data moves between devices by JAX's collectives and lax.ppermute only.
A program may use at most 128 MiB of HBM per device.

```python
import jax
import jax.numpy as jnp
from jax import lax

MODEL_WIDTH = 5376
QUERY_HEAD_COUNT = 16
KEY_VALUE_HEADS = 8
HEAD_SIZE = 128
QS = 168
LOOKBACK_WINDOW = 1024
TOK_DEV = 512
TOKEN_COUNT = 32768


def draw_tokens(key, part):
    sampled_values = jax.random.normal(jax.random.fold_in(key, 1), (TOKEN_COUNT, MODEL_WIDTH), jnp.float32)
    return jnp.clip(sampled_values, -8.0, 8.0).astype(jnp.bfloat16)


def draw_positions(key, part):
    jumps = jax.random.randint(jax.random.fold_in(key, 12), (TOKEN_COUNT,), 0, 8) == 0
    extra = jax.random.randint(jax.random.fold_in(key, 13), (TOKEN_COUNT,), 1, 4)
    step_sizes = 1 + jnp.where(jumps, extra, 0)
    relative = jnp.cumsum(step_sizes) - step_sizes[0]
    last_pos = 4 * TOKEN_COUNT - 1
    return (last_pos - relative[-1] + relative).astype(jnp.int32)


def grouped_query(key):
    sampled_values = jax.random.normal(jax.random.fold_in(key, 101), (MODEL_WIDTH, QUERY_HEAD_COUNT * HEAD_SIZE), jnp.float32)
    return jnp.clip(sampled_values, -6.0, 6.0) * MODEL_WIDTH ** (-0.5)


def draw_w_query(key, part):
    return grouped_query(key).astype(jnp.bfloat16)


def draw_key_matrix(key, part):
    sampled_values = jax.random.normal(jax.random.fold_in(key, 103), (MODEL_WIDTH, KEY_VALUE_HEADS * HEAD_SIZE), jnp.float32)
    return (jnp.clip(sampled_values, -6.0, 6.0) * MODEL_WIDTH ** (-0.5)).astype(jnp.bfloat16)


def draw_gain_query(key, part):
    sampled_values = jax.random.uniform(jax.random.fold_in(key, 202), (HEAD_SIZE,), jnp.float32, 0.5, 2.0)
    return sampled_values


def draw_gain_key(key, part):
    sampled_values = jax.random.uniform(jax.random.fold_in(key, 203), (HEAD_SIZE,), jnp.float32, 0.5, 2.0)
    return sampled_values


def level_of(key, extent, shards, smallest, high):
    def one(axis_at, blocks):
        draws = jax.random.uniform(jax.random.fold_in(jax.random.fold_in(key, 6), axis_at), (blocks,), jnp.float32, smallest / len(shards), high / len(shards))
        return jnp.repeat(jnp.exp(draws), extent[axis_at] // blocks).reshape((-1,) + (1,) * (len(extent) - axis_at - 1))

    factor_of = one(*shards[0])
    for cut in shards[1:]:
        factor_of = factor_of * one(*cut)
    return factor_of


def bell_draw(rng, shape, scale, limit, pieces=(), kind=jnp.bfloat16):
    array = jax.random.normal(rng, shape, jnp.float32) * scale
    if len(pieces) > 0:
        array = level_of(rng, shape, pieces, -0.22, 0.18) * array
    return jnp.clip(array, min=-limit, max=limit).astype(kind)


def setup_inputs(seed: int = 0) -> dict:
    key_list = jax.random.split(jax.random.key(seed), 11)
    tokens = draw_tokens(jax.random.fold_in(key_list[10], 71), 0)
    positions = draw_positions(jax.random.fold_in(key_list[10], 71), 0)
    w_query = draw_w_query(jax.random.fold_in(key_list[10], 71), 0)
    key_matrix = draw_key_matrix(jax.random.fold_in(key_list[10], 71), 0)
    value_matrix = bell_draw(key_list[4], (MODEL_WIDTH, KEY_VALUE_HEADS * HEAD_SIZE), MODEL_WIDTH ** -0.5, 0.078125, ((0, 64), (1, 4)))
    w_out = bell_draw(key_list[5], (QUERY_HEAD_COUNT * HEAD_SIZE, MODEL_WIDTH), (QUERY_HEAD_COUNT * HEAD_SIZE) ** -0.5, 0.125, ((0, 4), (1, 64)))
    gain_in = jnp.clip(1.0 + 0.18 * jax.random.normal(key_list[6], (MODEL_WIDTH,), jnp.float32), 0.1, 1.9)
    gain_query = draw_gain_query(jax.random.fold_in(key_list[10], 71), 0)
    gain_key = draw_gain_key(jax.random.fold_in(key_list[10], 71), 0)
    gain_post = jnp.clip(1.0 + 0.18 * jax.random.normal(key_list[9], (MODEL_WIDTH,), jnp.float32), 0.1, 1.9)
    return {"tokens": tokens, "positions": positions, "w_query": w_query, "key_matrix": key_matrix, "value_matrix": value_matrix, "w_out": w_out, "gain_in": gain_in, "gain_query": gain_query, "gain_key": gain_key, "gain_post": gain_post}


EPSILON = 1e-06
ROPE_BASE = 10000.0

def row_norm(values, scales):
    mean_square = lax.optimization_barrier(jnp.mean(values * values, axis=-1, keepdims=True))
    return values * lax.rsqrt(mean_square + EPSILON) * scales

def rotate(head_rows, offsets):
    half_dim = head_rows.shape[-1] // 2
    frequency = ROPE_BASE ** (-(jnp.arange(half_dim, dtype=jnp.float32) * 2.0) / head_rows.shape[-1])
    angles = offsets.astype(jnp.float32)[:, None] * frequency[None, :]
    cosine = jnp.cos(angles)[:, None, :]
    sine_wave = jnp.sin(angles)[:, None, :]
    first_half = head_rows[..., :half_dim]
    second_half = head_rows[..., half_dim:]
    return jnp.concatenate([first_half * cosine - second_half * sine_wave, second_half * cosine + first_half * sine_wave], axis=-1)

def attend(query_matrix, projected_keys, projected_values, query_offsets, key_offsets, key_valid):
    scores = jnp.einsum('qkgd,skd->kgqs', query_matrix.astype(jnp.float32), projected_keys.astype(jnp.float32)) * QS ** (-0.5)
    position_gap = query_offsets[:, None] - key_offsets[None, :]
    allowed = key_valid[None, :] & (position_gap >= 0) & (position_gap < LOOKBACK_WINDOW)
    scores = jnp.where(allowed[None, None], scores, -1e+30)
    row_max = lax.optimization_barrier(jnp.max(scores, axis=-1, keepdims=True))
    weights = jnp.where(allowed[None, None], jnp.exp(scores - row_max), 0.0)
    totals = lax.optimization_barrier(jnp.sum(weights, axis=-1, keepdims=True))
    rounded = weights.astype(jnp.bfloat16)
    mixed = jnp.einsum('kgqs,skd->qkgd', rounded.astype(jnp.float32), projected_values.astype(jnp.float32))
    mixed = mixed / jnp.transpose(totals, (2, 0, 1, 3))
    return mixed.astype(jnp.bfloat16).reshape(query_matrix.shape[0], -1)

def reference(tokens, positions, w_query, key_matrix, value_matrix, w_out, gain_in, gain_query, gain_key, gain_post):
    normalized_rows = row_norm(tokens.astype(jnp.float32), gain_in).astype(jnp.bfloat16)
    offsets = positions - positions[0]
    query_raw = jnp.dot(normalized_rows, w_query, preferred_element_type=jnp.float32).reshape(TOKEN_COUNT, QUERY_HEAD_COUNT, HEAD_SIZE)
    unnormed_keys = jnp.dot(normalized_rows, key_matrix, preferred_element_type=jnp.float32).reshape(TOKEN_COUNT, KEY_VALUE_HEADS, HEAD_SIZE)
    projected_values = jnp.dot(normalized_rows, value_matrix, preferred_element_type=jnp.float32).astype(jnp.bfloat16).reshape(TOKEN_COUNT, KEY_VALUE_HEADS, HEAD_SIZE)
    query_matrix = rotate(row_norm(query_raw, gain_query), offsets).astype(jnp.bfloat16)
    projected_keys = rotate(row_norm(unnormed_keys, gain_key), offsets).astype(jnp.bfloat16)
    query_matrix = query_matrix.reshape(TOKEN_COUNT, KEY_VALUE_HEADS, QUERY_HEAD_COUNT // KEY_VALUE_HEADS, HEAD_SIZE)
    keys_with_padding = jnp.concatenate([jnp.zeros((LOOKBACK_WINDOW, KEY_VALUE_HEADS, HEAD_SIZE), jnp.bfloat16), projected_keys], axis=0)
    values_with_padding = jnp.concatenate([jnp.zeros((LOOKBACK_WINDOW, KEY_VALUE_HEADS, HEAD_SIZE), jnp.bfloat16), projected_values], axis=0)
    padded_offsets = jnp.concatenate([jnp.zeros((LOOKBACK_WINDOW,), jnp.int32), offsets.astype(jnp.int32)], axis=0)

    def one_block(block_index):
        block_begin = (block_index * TOK_DEV).astype(jnp.int32)
        query_block = lax.dynamic_slice_in_dim(query_matrix, block_begin, TOK_DEV, 0)
        query_offsets = lax.dynamic_slice_in_dim(offsets.astype(jnp.int32), block_begin, TOK_DEV, 0)
        key_block = lax.dynamic_slice_in_dim(keys_with_padding, block_begin, LOOKBACK_WINDOW + TOK_DEV, 0)
        value_block = lax.dynamic_slice_in_dim(values_with_padding, block_begin, LOOKBACK_WINDOW + TOK_DEV, 0)
        key_offsets = lax.dynamic_slice_in_dim(padded_offsets, block_begin, LOOKBACK_WINDOW + TOK_DEV, 0)
        key_valid = block_begin + jnp.arange(LOOKBACK_WINDOW + TOK_DEV, dtype=jnp.int32) >= LOOKBACK_WINDOW
        return attend(query_block, key_block, value_block, query_offsets, key_offsets, key_valid)
    blocks = lax.map(one_block, jnp.arange(TOKEN_COUNT // TOK_DEV, dtype=jnp.int32))
    attended = blocks.reshape(TOKEN_COUNT, QUERY_HEAD_COUNT * HEAD_SIZE)
    projected = jnp.dot(attended, w_out, preferred_element_type=jnp.float32)
    return (tokens.astype(jnp.float32) + row_norm(projected, gain_post)).astype(jnp.bfloat16)
```

```python
import functools

import jax
import jax.numpy as jnp
from jax import lax
from jax.experimental import pallas as pl
from jax.experimental.pallas import tpu as pltpu
from jax.sharding import PartitionSpec as P

HEAD_SIZE = 128
QS = 168
LOOKBACK_WINDOW = 1024
EPSILON = 1e-06
ROPE_BASE = 10000.0
Z, Y, C, X = 8, 4, 2, 4
BLOCK = 512
PAIR = 1024
VMEM = pltpu.VMEM
MIB = 1024 * 1024


def ctx_pairs(move):
    pairs = []
    for source in range(Z * Y * C):
        target = move(source // (Y * C), source // C % Y, source % C)
        if target is not None:
            z, y, c = target
            pairs.append((source, (z % Z) * Y * C + (y % Y) * C + c))
    return pairs


def swap_cores(value):
    return lax.ppermute(value, "ctx", ctx_pairs(lambda z, y, c: (z, y, 1 - c)))


def shift_x(value, steps):
    return lax.ppermute(value, "tp", [(x, (x + steps) % X) for x in range(X)])


def next_pair(value):
    pairs = [(source, source + C) for source in range(Z * Y * C - C)]
    return lax.ppermute(value, "ctx", pairs)


PLANES = [[z * Y * C + y * C + c for z in range(Z) for y in range(Y)] for c in range(C)]


def norm_body(rows_ref, gain_ref, out_ref):
    rows = rows_ref[...].astype(jnp.float32)
    scale = lax.rsqrt(jnp.mean(rows * rows, axis=-1, keepdims=True) + EPSILON)
    out_ref[...] = (rows * scale * gain_ref[...]).astype(jnp.bfloat16)


def input_norm(rows, gain):
    count, width = rows.shape
    step = 32
    return pl.pallas_call(
        norm_body,
        grid=(count // step,),
        in_specs=[
            pl.BlockSpec((step, width), lambda i: (i, 0)),
            pl.BlockSpec((1, width), lambda i: (0, 0)),
        ],
        out_specs=pl.BlockSpec((step, width), lambda i: (i, 0)),
        out_shape=jax.ShapeDtypeStruct(rows.shape, jnp.bfloat16),
        name="input_norm",
    )(rows, gain.reshape(1, width))


def head_norm_rope(raw, gain, cosine, sine):
    scale = lax.rsqrt(jnp.mean(raw * raw, axis=-1, keepdims=True) + EPSILON)
    normed = raw * scale * gain
    return normed * cosine + pltpu.roll(normed, HEAD_SIZE // 2, 1) * sine


def project_body(kinds, place_ref, *refs):
    pieces = refs[:10]
    weight_ref, gain_ref, cos_ref, sin_ref, out_ref, rows_ref, sems = refs[10:]
    x, c = place_ref[0], place_ref[1]
    quarter, half = BLOCK // X, BLOCK // X // 2
    copies = []
    for side in range(2):
        core = c if side == 0 else 1 - c
        own = pieces[5 * side : 5 * side + 5]
        for k, (piece, rel, shift, size) in enumerate(
            [
                (own[0], 0, 0, quarter),
                (own[1], 1, 0, quarter),
                (own[2], 2, 0, half),
                (own[3], 2, half, half),
                (own[4], 3, 0, quarter),
            ]
        ):
            start = pl.multiple_of(core * BLOCK + lax.rem(x + rel, X) * quarter + shift, half)
            copies.append(
                pltpu.make_async_copy(piece, rows_ref.at[pl.ds(start, size)], sems.at[5 * side + k])
            )
    for copy in copies:
        copy.start()
    for side in range(2):
        for copy in copies[5 * side : 5 * side + 5]:
            copy.wait()
        core = c if side == 0 else 1 - c
        start = pl.multiple_of(core * BLOCK, BLOCK)
        raw = jnp.dot(
            rows_ref[pl.ds(start, BLOCK), :], weight_ref[...], preferred_element_type=jnp.float32
        )
        for h, kind in enumerate(kinds):
            head = raw[:, h * HEAD_SIZE : (h + 1) * HEAD_SIZE]
            if kind == "rope":
                head = head_norm_rope(
                    head, gain_ref[...], cos_ref[pl.ds(start, BLOCK), :], sin_ref[pl.ds(start, BLOCK), :]
                )
            out_ref[h, pl.ds(start, BLOCK), :] = head.astype(jnp.bfloat16)


def project(kinds, place, pieces, gathered, column, gain, cosine, sine, name):
    width = gathered.shape[0]
    whole = lambda shape: pl.BlockSpec(shape, lambda i, p: (0,) * len(shape))
    return pl.pallas_call(
        functools.partial(project_body, kinds),
        grid_spec=pltpu.PrefetchScalarGridSpec(
            num_scalar_prefetch=1,
            grid=(1,),
            in_specs=[pl.BlockSpec(memory_space=pl.ANY)] * 10
            + [
                pl.BlockSpec((width, 2 * HEAD_SIZE), lambda i, p: (0, column)),
                whole((1, HEAD_SIZE)),
                whole((PAIR, HEAD_SIZE)),
                whole((PAIR, HEAD_SIZE)),
            ],
            out_specs=whole((2, PAIR, HEAD_SIZE)),
            scratch_shapes=[
                pltpu.VMEM((PAIR, width), jnp.bfloat16),
                pltpu.SemaphoreType.DMA((10,)),
            ],
        ),
        out_shape=jax.ShapeDtypeStruct((2, PAIR, HEAD_SIZE), jnp.bfloat16),
        compiler_params=pltpu.CompilerParams(vmem_limit_bytes=40 * MIB),
        cost_estimate=pl.CostEstimate(
            flops=2 * PAIR * width * 256, bytes_accessed=14 * MIB, transcendentals=0
        ),
        name=name,
    )(place, *pieces, gathered, gain.reshape(1, HEAD_SIZE), cosine, sine)


TILE = 256


def attend_body(q_ref, own_ref, prev_ref, qoff_ref, koff_ref, out_ref):
    for tile in range(PAIR // TILE):
        first, last = tile * TILE, (tile + 1) * TILE
        keys = jnp.concatenate([prev_ref[0, first:], own_ref[0, :last]], axis=0)
        values = jnp.concatenate([prev_ref[1, first:], own_ref[1, :last]], axis=0)
        span = PAIR + TILE
        gap = qoff_ref[first:last, :] - koff_ref[:, first : first + span]
        allowed = (gap >= 0) & (gap < LOOKBACK_WINDOW)
        for h in range(2):
            scores = lax.dot_general(
                q_ref[h, first:last],
                keys,
                (((1,), (1,)), ((), ())),
                preferred_element_type=jnp.float32,
            ) * QS ** (-0.5)
            scores = jnp.where(allowed, scores, -1e30)
            row_max = jnp.max(scores, axis=-1, keepdims=True)
            weights = jnp.exp(scores - row_max)
            totals = jnp.sum(weights, axis=-1, keepdims=True)
            mixed = jnp.dot(
                weights.astype(jnp.bfloat16), values, preferred_element_type=jnp.float32
            )
            out_ref[first:last, h * HEAD_SIZE : (h + 1) * HEAD_SIZE] = (mixed / totals).astype(
                jnp.bfloat16
            )


def attend(queries, own, prev, query_offsets, key_offsets):
    return pl.pallas_call(
        attend_body,
        out_shape=jax.ShapeDtypeStruct((PAIR, 2 * HEAD_SIZE), jnp.bfloat16),
        compiler_params=pltpu.CompilerParams(vmem_limit_bytes=32 * MIB),
        cost_estimate=pl.CostEstimate(
            flops=4 * PAIR * 1280 * 256, bytes_accessed=3 * MIB, transcendentals=2 * PAIR * 1280
        ),
        name="attend",
    )(queries, own, prev, query_offsets, key_offsets)


def out_body(low_ref, high_ref, wlow_ref, whigh_ref, out_ref):
    nt = (((1,), (1,)), ((), ()))
    total = lax.dot_general(low_ref[...], wlow_ref[...], nt, preferred_element_type=jnp.float32)
    total += lax.dot_general(high_ref[...], whigh_ref[...], nt, preferred_element_type=jnp.float32)
    out_ref[...] = total.astype(jnp.bfloat16)


def out_project(own, other, own_weights, other_weights):
    width = own_weights.shape[0]
    step = 768
    return pl.pallas_call(
        out_body,
        grid=(width // step,),
        in_specs=[
            pl.BlockSpec((BLOCK, 256), lambda i: (0, 0)),
            pl.BlockSpec((BLOCK, 256), lambda i: (0, 0)),
            pl.BlockSpec((step, 256), lambda i: (i, 0)),
            pl.BlockSpec((step, 256), lambda i: (i, 0)),
        ],
        out_specs=pl.BlockSpec((BLOCK, step), lambda i: (0, i)),
        out_shape=jax.ShapeDtypeStruct((BLOCK, width), jnp.bfloat16),
        cost_estimate=pl.CostEstimate(
            flops=2 * BLOCK * width * 512, bytes_accessed=12 * MIB, transcendentals=0
        ),
        name="out_project",
    )(own, other, own_weights, other_weights)


def final_body(sum_ref, rows_ref, gain_ref, out_ref):
    summed = sum_ref[...].astype(jnp.float32)
    scale = lax.rsqrt(jnp.mean(summed * summed, axis=-1, keepdims=True) + EPSILON)
    out = rows_ref[...].astype(jnp.float32) + summed * scale * gain_ref[...]
    out_ref[...] = out.astype(jnp.bfloat16)


def final_norm(summed, rows, gain):
    count, width = rows.shape
    step = 32
    block = pl.BlockSpec((step, width), lambda i: (i, 0))
    return pl.pallas_call(
        final_body,
        grid=(count // step,),
        in_specs=[block, block, pl.BlockSpec((1, width), lambda i: (0, 0))],
        out_specs=block,
        out_shape=jax.ShapeDtypeStruct(rows.shape, jnp.bfloat16),
        name="final_norm",
    )(summed, rows, gain.reshape(1, width))


def core_order(first, second, c):
    low = jnp.where(c == 0, first, second)
    high = jnp.where(c == 0, second, first)
    return low, high


def shards(
    tokens,
    positions,
    w_query,
    key_matrix,
    value_matrix,
    w_out,
    gain_in,
    gain_query,
    gain_key,
    gain_post,
):
    ctx = lax.axis_index("ctx")
    c, pair = ctx % C, ctx // C
    x = lax.axis_index("tp")
    place = jnp.stack([x, c]).astype(jnp.int32)

    out_rows = w_out.T
    sides = [
        jnp.concatenate(
            [
                w_query[:, side * 256 : side * 256 + 256],
                key_matrix[:, side * 128 : side * 128 + 128],
                value_matrix[:, side * 128 : side * 128 + 128],
                out_rows[:, side * 256 : side * 256 + 256],
            ],
            axis=1,
        )
        for side in range(2)
    ]
    mine, theirs = core_order(sides[0], sides[1], c)
    received = swap_cores(theirs)
    stacked = jnp.concatenate(core_order(mine, received, c), axis=0)
    gathered = lax.all_gather(stacked, "ctx", axis=0, tiled=True, axis_index_groups=PLANES)

    rows = input_norm(tokens, gain_in)
    from_low, from_high = shift_x(rows, 1), shift_x(rows, -1)
    half = rows.shape[0] // 2
    far_low = shift_x(from_low[:half], 1)
    far_high = shift_x(from_high[half:], -1)
    pieces = [rows, from_high, far_low, far_high, from_low]
    pieces = pieces + [swap_cores(piece) for piece in pieces]

    offsets = positions - positions[0]
    start = pair * PAIR
    query_offsets = lax.dynamic_slice_in_dim(offsets, start, PAIR, 0)
    padded = jnp.concatenate([jnp.full((PAIR,), -(2**30), jnp.int32), offsets])
    key_offsets = lax.dynamic_slice_in_dim(padded, start, 2 * PAIR, 0)
    half_dim = HEAD_SIZE // 2
    frequency = ROPE_BASE ** (-(jnp.arange(half_dim, dtype=jnp.float32) * 2.0) / HEAD_SIZE)
    angles = query_offsets.astype(jnp.float32)[:, None] * frequency[None, :]
    cosine, sine = jnp.cos(angles), jnp.sin(angles)
    cosine = jnp.concatenate([cosine, cosine], axis=1)
    sine = jnp.concatenate([-sine, sine], axis=1)

    own = project(
        ("rope", "plain"), place, pieces, gathered, 1, gain_key, cosine, sine, "kv_project"
    )
    prev = next_pair(own)
    queries = project(
        ("rope", "rope"), place, pieces, gathered, 0, gain_query, cosine, sine, "q_project"
    )
    own_weights = gathered[:, 512:]
    other_weights = swap_cores(own_weights)
    attended = attend(queries, own, prev, query_offsets[:, None], key_offsets[None, :])
    keep = lax.dynamic_slice_in_dim(attended, c * BLOCK, BLOCK, 0)
    give = lax.dynamic_slice_in_dim(attended, (1 - c) * BLOCK, BLOCK, 0)
    other = swap_cores(give)
    projected = out_project(keep, other, own_weights, other_weights)
    summed = lax.psum_scatter(projected, "tp", scatter_dimension=0, tiled=True)
    return final_norm(summed, tokens, gain_post)


def solution(mesh):
    in_specs = (
        P(("ctx", "tp"), None),
        P(),
        P("ctx", "tp"),
        P("ctx", "tp"),
        P("ctx", "tp"),
        P("tp", "ctx"),
        P(),
        P(),
        P(),
        P(),
    )
    out_specs = P(("ctx", "tp"), None)
    return jax.shard_map(shards, mesh=mesh, in_specs=in_specs, out_specs=out_specs, check_vma=False)
```

```python
import functools

import jax
import jax.numpy as jnp
from jax import lax
from jax.experimental import pallas as pl
from jax.experimental.pallas import tpu as pltpu
from jax.sharding import PartitionSpec as P

HEAD_SIZE = 128
QS = 168
LOOKBACK_WINDOW = 1024
EPSILON = 1e-06
ROPE_BASE = 10000.0
Z, Y, C, X = 8, 4, 2, 4
BLOCK = 512
PAIR = 1024
VMEM = pltpu.VMEM
MIB = 1024 * 1024


def ctx_pairs(move):
    pairs = []
    for source in range(Z * Y * C):
        target = move(source // (Y * C), source // C % Y, source % C)
        if target is not None:
            z, y, c = target
            pairs.append((source, (z % Z) * Y * C + (y % Y) * C + c))
    return pairs


def swap_cores(value):
    return lax.ppermute(value, "ctx", ctx_pairs(lambda z, y, c: (z, y, 1 - c)))


def shift_x(value, steps):
    return lax.ppermute(value, "tp", [(x, (x + steps) % X) for x in range(X)])


def next_pair(value):
    pairs = [(source, source + C) for source in range(Z * Y * C - C)]
    return lax.ppermute(value, "ctx", pairs)


def shift_y(value, steps):
    return lax.ppermute(value, "ctx", ctx_pairs(lambda z, y, c: (z, y + steps, c)))


def shift_z(value, steps):
    return lax.ppermute(value, "ctx", ctx_pairs(lambda z, y, c: (z + steps, y, c)))


def trade_x_z(value):
    pairs = []
    for source in range(Z * Y * C * X):
        ctx, x = source // X, source % X
        z, rest = ctx // (Y * C), ctx % (Y * C)
        pairs.append((source, ((x * 2 + z % 2) * Y * C + rest) * X + z // 2))
    return lax.ppermute(value, ("ctx", "tp"), pairs)


def together(*values):
    return lax.optimization_barrier(values)


ROWS = [[z * Y * C + y * C + c for y in range(Y)] for z in range(Z) for c in range(C)]
COLUMNS = [[z * Y * C + y * C + c for z in range(Z)] for y in range(Y) for c in range(C)]


def norm_body(rows_ref, gain_ref, out_ref):
    rows = rows_ref[...].astype(jnp.float32)
    scale = lax.rsqrt(jnp.mean(rows * rows, axis=-1, keepdims=True) + EPSILON)
    out_ref[...] = (rows * scale * gain_ref[...]).astype(jnp.bfloat16)


def input_norm(rows, gain):
    count, width = rows.shape
    step = 32
    return pl.pallas_call(
        norm_body,
        grid=(count // step,),
        in_specs=[
            pl.BlockSpec((step, width), lambda i: (i, 0)),
            pl.BlockSpec((1, width), lambda i: (0, 0)),
        ],
        out_specs=pl.BlockSpec((step, width), lambda i: (i, 0)),
        out_shape=jax.ShapeDtypeStruct(rows.shape, jnp.bfloat16),
        name="input_norm",
    )(rows, gain.reshape(1, width))


def head_norm_rope(raw, gain, cosine, sine):
    scale = lax.rsqrt(jnp.mean(raw * raw, axis=-1, keepdims=True) + EPSILON)
    normed = raw * scale * gain
    return normed * cosine + pltpu.roll(normed, HEAD_SIZE // 2, 1) * sine


PARTS = 3


def project_body(
    mine, place_ref, rows_hbm, weight_hbm, gq_ref, gk_ref, cos_ref, sin_ref,
    q_ref, kv_ref, rows_ref, weight_ref, total_ref, sems,
):
    c = place_ref[3]
    start = pl.multiple_of((c if mine else 1 - c) * BLOCK, BLOCK)
    step = rows_ref.shape[1] // PARTS
    copies = []
    for k in range(PARTS):
        span = pl.ds(k * step, step)
        copies.append(
            (
                pltpu.make_async_copy(rows_hbm.at[:, span], rows_ref.at[:, span], sems.at[2 * k]),
                pltpu.make_async_copy(
                    weight_hbm.at[span], weight_ref.at[span], sems.at[2 * k + 1]
                ),
            )
        )
    for pair in copies:
        for copy in pair:
            copy.start()
    for k, pair in enumerate(copies):
        for copy in pair:
            copy.wait()
        span = slice(k * step, (k + 1) * step)
        part = jnp.dot(
            rows_ref[:, span], weight_ref[span, :], preferred_element_type=jnp.float32
        )
        if k == 0:
            total_ref[...] = part
        else:
            total_ref[...] += part
    cosine, sine = cos_ref[pl.ds(start, BLOCK), :], sin_ref[pl.ds(start, BLOCK), :]
    heads = [total_ref[:, h * HEAD_SIZE : (h + 1) * HEAD_SIZE] for h in range(4)]
    kv_ref[0] = head_norm_rope(heads[2], gk_ref[...], cosine, sine).astype(jnp.bfloat16)
    kv_ref[1] = heads[3].astype(jnp.bfloat16)
    for h in range(2):
        q_ref[h] = head_norm_rope(heads[h], gq_ref[...], cosine, sine).astype(jnp.bfloat16)


def whole(shape):
    return pl.BlockSpec(shape, lambda i, p: (0,) * len(shape))


SMEM = pl.BlockSpec(memory_space=pltpu.SMEM)
HBM = pl.BlockSpec(memory_space=pltpu.HBM)
HELD = pl.BlockSpec(memory_space=pltpu.VMEM)


def project(mine, place, rows, weights, tables, name):
    width = weights.shape[0]
    head = jax.ShapeDtypeStruct((2, BLOCK, HEAD_SIZE), jnp.bfloat16)
    return pl.pallas_call(
        functools.partial(project_body, mine),
        in_specs=[SMEM, HBM, HBM] + [HELD] * 4,
        out_specs=[HELD] * 2,
        out_shape=[head] * 2,
        scratch_shapes=[
            pltpu.VMEM((BLOCK, width), jnp.bfloat16),
            pltpu.VMEM((width, 512), jnp.bfloat16),
            pltpu.VMEM((BLOCK, 512), jnp.float32),
            pltpu.SemaphoreType.DMA((2 * PARTS,)),
        ],
        compiler_params=pltpu.CompilerParams(vmem_limit_bytes=60 * MIB),
        cost_estimate=pl.CostEstimate(
            flops=2 * BLOCK * width * 512, bytes_accessed=12 * MIB, transcendentals=0
        ),
        name=name,
    )(place, rows, weights, *tables)


def rows_body(place_ref, *refs):
    pieces, out_ref = refs[:5], refs[5]
    x = place_ref[0]
    quarter, half = BLOCK // X, BLOCK // X // 2
    plan = [(0, 0, quarter), (1, 0, quarter), (2, 0, half), (2, half, half), (3, 0, quarter)]
    for piece, (rel, shift, size) in zip(pieces, plan):
        at = pl.multiple_of(lax.rem(x + rel, X) * quarter + shift, half)
        out_ref[pl.ds(at, size), :] = piece[...]


def place_rows(place, pieces):
    width = pieces[0].shape[1]
    step = 768
    return pl.pallas_call(
        rows_body,
        grid_spec=pltpu.PrefetchScalarGridSpec(
            num_scalar_prefetch=1,
            grid=(width // step,),
            in_specs=[pl.BlockSpec((p.shape[0], step), lambda i, p: (0, i)) for p in pieces],
            out_specs=pl.BlockSpec((BLOCK, step), lambda i, p: (0, i)),
        ),
        out_shape=jax.ShapeDtypeStruct((BLOCK, width), jnp.bfloat16),
        cost_estimate=pl.CostEstimate(flops=0, bytes_accessed=11 * MIB, transcendentals=0),
        name="place_rows",
    )(place, *pieces)


TILE = 256
SPAN = PAIR + TILE


def attend_body(mine, place_ref, q_ref, first_ref, second_ref, pfirst_ref, psecond_ref, qoff_ref, koff_ref, out_ref, keys_ref, values_ref):
    c = place_ref[3]
    for base, refs in ((0, (pfirst_ref, psecond_ref)), (PAIR, (first_ref, second_ref))):
        for block, ref in ((c, refs[0]), (1 - c, refs[1])):
            at = pl.multiple_of(base + block * BLOCK, BLOCK)
            keys_ref[pl.ds(at, BLOCK), :] = ref[0]
            values_ref[pl.ds(at, BLOCK), :] = ref[1]
    block = c if mine else 1 - c
    for tile in range(BLOCK // TILE):
        first, last = tile * TILE, (tile + 1) * TILE
        at = pl.multiple_of(block * BLOCK + first, TILE)
        keys = keys_ref[pl.ds(at, SPAN), :]
        values = values_ref[pl.ds(at, SPAN), :]
        gap = qoff_ref[pl.ds(at, TILE), :] - koff_ref[pl.ds(block * (BLOCK // TILE) + tile, 1), :]
        allowed = (gap >= 0) & (gap < LOOKBACK_WINDOW)
        for h in range(2):
            scores = lax.dot_general(
                q_ref[h, first:last],
                keys,
                (((1,), (1,)), ((), ())),
                preferred_element_type=jnp.float32,
            ) * QS ** (-0.5)
            scores = jnp.where(allowed, scores, -1e30)
            row_max = jnp.max(scores, axis=-1, keepdims=True)
            weights = jnp.exp(scores - row_max)
            totals = jnp.sum(weights, axis=-1, keepdims=True)
            mixed = jnp.dot(
                weights.astype(jnp.bfloat16), values, preferred_element_type=jnp.float32
            )
            out_ref[first:last, h * HEAD_SIZE : (h + 1) * HEAD_SIZE] = (mixed / totals).astype(
                jnp.bfloat16
            )


def attend(mine, place, queries, blocks, query_offsets, key_offsets, name):
    pair_block = whole((2, BLOCK, HEAD_SIZE))
    return pl.pallas_call(
        functools.partial(attend_body, mine),
        grid_spec=pltpu.PrefetchScalarGridSpec(
            num_scalar_prefetch=1,
            grid=(1,),
            in_specs=[pair_block] * 5
            + [whole((PAIR, 1)), whole((PAIR // TILE, SPAN))],
            out_specs=whole((BLOCK, 2 * HEAD_SIZE)),
            scratch_shapes=[pltpu.VMEM((2 * PAIR, HEAD_SIZE), jnp.bfloat16)] * 2,
        ),
        out_shape=jax.ShapeDtypeStruct((BLOCK, 2 * HEAD_SIZE), jnp.bfloat16),
        compiler_params=pltpu.CompilerParams(vmem_limit_bytes=32 * MIB),
        cost_estimate=pl.CostEstimate(
            flops=4 * BLOCK * SPAN * 256, bytes_accessed=3 * MIB, transcendentals=2 * BLOCK * SPAN
        ),
        name=name,
    )(place, queries, *blocks, query_offsets, key_offsets)


def out_body(place_ref, *refs):
    pieces, (own_ref, other_ref, *outs) = refs[:8], refs[8:]
    rows_ref, weight_ref, sems = outs[X:]
    x = place_ref[0]
    quarter = BLOCK // X
    count = own_ref.shape[0] // X
    copies = []
    for k in range(X):
        at = pl.multiple_of(lax.rem(x + k, X) * count, 16)
        for side, ref in enumerate((own_ref, other_ref)):
            slot = 2 * k + side
            copies.append(
                pltpu.make_async_copy(
                    ref.at[pl.ds(at, count)], weight_ref.at[slot], sems.at[slot]
                )
            )
    for copy in copies:
        copy.start()
    for k, piece in enumerate(pieces):
        for rel in range(X):
            at = pl.multiple_of(lax.rem(x + rel, X) * quarter, quarter)
            rows_ref[rel * quarter : (rel + 1) * quarter, k * 256 : (k + 1) * 256] = piece[
                pl.ds(at, quarter), :
            ]
    for copy in copies:
        copy.wait()
    weights = jnp.concatenate([weight_ref[k] for k in range(2 * X)], axis=1)
    total = lax.dot_general(
        rows_ref[...], weights, (((1,), (1,)), ((), ())), preferred_element_type=jnp.float32
    )
    for rel, out_ref in enumerate(outs[:X]):
        out_ref[...] = total[rel * quarter : (rel + 1) * quarter].astype(jnp.bfloat16)


def out_project(place, pieces, own, other):
    count = own.shape[0] // X
    chunk = jax.ShapeDtypeStruct((BLOCK // X, count), jnp.bfloat16)
    return pl.pallas_call(
        out_body,
        in_specs=[SMEM] + [HELD] * 8 + [HBM] * 2,
        out_specs=[HELD] * X,
        out_shape=[chunk] * X,
        scratch_shapes=[
            pltpu.VMEM((BLOCK, 2048), jnp.bfloat16),
            pltpu.VMEM((2 * X, count, 256), jnp.bfloat16),
            pltpu.SemaphoreType.DMA((2 * X,)),
        ],
        compiler_params=pltpu.CompilerParams(vmem_limit_bytes=60 * MIB),
        cost_estimate=pl.CostEstimate(
            flops=2 * BLOCK * count * 2048, bytes_accessed=9 * MIB, transcendentals=0
        ),
        name="out_project",
    )(place, *pieces, own, other)


def final_body(place_ref, *refs):
    pieces, (rows_ref, gain_ref, out_ref, stage_ref) = refs[:X], refs[X:]
    x = place_ref[0]
    for k, piece in enumerate(pieces):
        stage_ref[lax.rem(x + k, X)] = piece[...]
    step = 32
    for at in range(0, rows_ref.shape[0], step):
        summed = jnp.concatenate(
            [stage_ref[k, at : at + step].astype(jnp.float32) for k in range(X)], axis=1
        )
        scale = lax.rsqrt(jnp.mean(summed * summed, axis=-1, keepdims=True) + EPSILON)
        out = rows_ref[at : at + step].astype(jnp.float32) + summed * scale * gain_ref[...]
        out_ref[at : at + step] = out.astype(jnp.bfloat16)


def final_norm(place, pieces, rows, gain):
    width = rows.shape[1]
    return pl.pallas_call(
        final_body,
        in_specs=[SMEM] + [HELD] * (X + 2),
        out_specs=HELD,
        out_shape=jax.ShapeDtypeStruct(rows.shape, jnp.bfloat16),
        scratch_shapes=[pltpu.VMEM((X, rows.shape[0], width // X), jnp.bfloat16)],
        compiler_params=pltpu.CompilerParams(vmem_limit_bytes=32 * MIB),
        name="final_norm",
    )(place, *pieces, rows, gain.reshape(1, width))


def core_order(first, second, c):
    low = jnp.where(c == 0, first, second)
    high = jnp.where(c == 0, second, first)
    return low, high


def shards(
    tokens,
    positions,
    w_query,
    key_matrix,
    value_matrix,
    w_out,
    gain_in,
    gain_query,
    gain_key,
    gain_post,
):
    ctx = lax.axis_index("ctx")
    c, y, z, pair = ctx % C, ctx // C % Y, ctx // (Y * C), ctx // C
    x = lax.axis_index("tp")
    place = jnp.stack([x, y, z, c]).astype(jnp.int32)
    width = tokens.shape[1]

    out_rows = w_out.T
    sides = [
        jnp.concatenate(
            [
                w_query[:, side * 256 : side * 256 + 256],
                key_matrix[:, side * 128 : side * 128 + 128],
                value_matrix[:, side * 128 : side * 128 + 128],
                out_rows[:, side * 256 : side * 256 + 256],
            ],
            axis=1,
        )
        for side in range(2)
    ]
    mine, theirs = core_order(sides[0], sides[1], c)
    received = swap_cores(theirs)
    stacked = jnp.concatenate(core_order(mine, received, c), axis=0)
    part, part_out = stacked[:, :512], trade_x_z(stacked[:, 512:])
    part = lax.all_gather(part, "ctx", axis=0, tiled=True, axis_index_groups=ROWS)
    part, moving = together(part, tokens)
    weights = lax.all_gather(part, "ctx", axis=0, tiled=True, axis_index_groups=COLUMNS)

    start = pair * PAIR
    query_offsets = lax.dynamic_slice_in_dim(positions, start, PAIR, 0) - positions[0]
    before = lax.dynamic_slice_in_dim(positions, jnp.maximum(start - PAIR, 0), PAIR, 0)
    before = jnp.where(pair == 0, -(2**30), before - positions[0])
    key_offsets = jnp.concatenate([before, query_offsets])
    key_offsets = jnp.stack([key_offsets[at : at + SPAN] for at in range(0, PAIR, TILE)])
    half_dim = HEAD_SIZE // 2
    frequency = ROPE_BASE ** (-(jnp.arange(half_dim, dtype=jnp.float32) * 2.0) / HEAD_SIZE)
    angles = query_offsets.astype(jnp.float32)[:, None] * frequency[None, :]
    cosine, sine = jnp.cos(angles), jnp.sin(angles)
    cosine = jnp.concatenate([cosine, cosine], axis=1)
    sine = jnp.concatenate([-sine, sine], axis=1)
    query_offsets = query_offsets[:, None]

    rows = input_norm(moving, gain_in)
    from_low, from_high = shift_x(rows, 1), shift_x(rows, -1)
    part_out = lax.all_gather(part_out, "ctx", axis=0, tiled=True, axis_index_groups=ROWS)
    from_low, from_high, part_out, cosine, sine, query_offsets, key_offsets = together(
        from_low, from_high, part_out, cosine, sine, query_offsets, key_offsets
    )
    half = rows.shape[0] // 2
    far_low = shift_x(from_low[:half], 1)
    far_high = shift_x(from_high[half:], -1)
    own_rows = place_rows(place, [rows, from_high, far_low, far_high, from_low])
    other_rows = swap_cores(own_rows)

    tables = [gain_query.reshape(1, HEAD_SIZE), gain_key.reshape(1, HEAD_SIZE), cosine, sine]

    weights, part_out = together(weights, part_out)
    own_out = lax.all_gather(part_out, "ctx", axis=0, tiled=True, axis_index_groups=COLUMNS)
    q_own, kv_own = project(True, place, own_rows, weights, tables, "project_own")
    prev_own = next_pair(kv_own)
    q_other, kv_other = project(False, place, other_rows, weights, tables, "project_other")
    prev_other = next_pair(kv_other)
    blocks = [kv_own, kv_other, prev_own, prev_other]
    keep = attend(True, place, q_own, blocks, query_offsets, key_offsets, "attend_keep")
    q_other, keep = together(q_other, keep)
    give = attend(False, place, q_other, blocks, query_offsets, key_offsets, "attend_give")
    far_keep = [shift_x(keep, -1), shift_x(keep, 2), shift_x(keep, 1)]
    other = swap_cores(give)
    far_other = [shift_x(other, -1), shift_x(other, 2), shift_x(other, 1)]
    own_out, *far_keep = together(own_out, *far_keep)
    other_out = swap_cores(own_out)
    attended = [keep, other]
    for k in range(3):
        attended += [far_keep[k], far_other[k]]
    sums = out_project(place, attended, own_out, other_out)
    sums = [sums[0], shift_x(sums[3], -1), shift_x(sums[2], 2), shift_x(sums[1], 1)]
    return final_norm(place, sums, tokens, gain_post)


def solution(mesh):
    in_specs = (
        P(("ctx", "tp"), None),
        P(),
        P("ctx", "tp"),
        P("ctx", "tp"),
        P("ctx", "tp"),
        P("tp", "ctx"),
        P(),
        P(),
        P(),
        P(),
    )
    out_specs = P(("ctx", "tp"), None)
    return jax.shard_map(shards, mesh=mesh, in_specs=in_specs, out_specs=out_specs, check_vma=False)
```

```python
import functools

import jax
import jax.numpy as jnp
from jax import lax
from jax.experimental import pallas as pl
from jax.experimental.pallas import tpu as pltpu
from jax.sharding import PartitionSpec as P

HEAD_SIZE = 128
QS = 168
LOOKBACK_WINDOW = 1024
EPSILON = 1e-06
ROPE_BASE = 10000.0
Z, Y, C, X = 8, 4, 2, 4
BLOCK = 512
PAIR = 1024
VMEM = pltpu.VMEM
MIB = 1024 * 1024


def ctx_pairs(move):
    pairs = []
    for source in range(Z * Y * C):
        target = move(source // (Y * C), source // C % Y, source % C)
        if target is not None:
            z, y, c = target
            pairs.append((source, (z % Z) * Y * C + (y % Y) * C + c))
    return pairs


def swap_cores(value):
    return lax.ppermute(value, "ctx", ctx_pairs(lambda z, y, c: (z, y, 1 - c)))


def shift_x(value, steps):
    return lax.ppermute(value, "tp", [(x, (x + steps) % X) for x in range(X)])


def next_pair(value):
    pairs = [(source, source + C) for source in range(Z * Y * C - C)]
    return lax.ppermute(value, "ctx", pairs)


def shift_y(value, steps):
    return lax.ppermute(value, "ctx", ctx_pairs(lambda z, y, c: (z, y + steps, c)))


def shift_z(value, steps):
    return lax.ppermute(value, "ctx", ctx_pairs(lambda z, y, c: (z + steps, y, c)))


def trade_x_z(value):
    pairs = []
    for source in range(Z * Y * C * X):
        ctx, x = source // X, source % X
        z, rest = ctx // (Y * C), ctx % (Y * C)
        pairs.append((source, ((x * 2 + z % 2) * Y * C + rest) * X + z // 2))
    return lax.ppermute(value, ("ctx", "tp"), pairs)


def together(*values):
    return lax.optimization_barrier(values)


ROWS = [[z * Y * C + y * C + c for y in range(Y)] for z in range(Z) for c in range(C)]
COLUMNS = [[z * Y * C + y * C + c for z in range(Z)] for y in range(Y) for c in range(C)]


def norm_body(rows_ref, gain_ref, out_ref):
    rows = rows_ref[...].astype(jnp.float32)
    scale = lax.rsqrt(jnp.mean(rows * rows, axis=-1, keepdims=True) + EPSILON)
    out_ref[...] = (rows * scale * gain_ref[...]).astype(jnp.bfloat16)


def input_norm(rows, gain):
    count, width = rows.shape
    step = 32
    return pl.pallas_call(
        norm_body,
        grid=(count // step,),
        in_specs=[
            pl.BlockSpec((step, width), lambda i: (i, 0)),
            pl.BlockSpec((1, width), lambda i: (0, 0)),
        ],
        out_specs=pl.BlockSpec((step, width), lambda i: (i, 0)),
        out_shape=jax.ShapeDtypeStruct(rows.shape, jnp.bfloat16),
        name="input_norm",
    )(rows, gain.reshape(1, width))


def head_norm_rope(raw, gain, cosine, sine):
    scale = lax.rsqrt(jnp.mean(raw * raw, axis=-1, keepdims=True) + EPSILON)
    normed = raw * scale * gain
    return normed * cosine + pltpu.roll(normed, HEAD_SIZE // 2, 1) * sine


PARTS = 3


def project_body(
    mine, place_ref, rows_hbm, weight_hbm, gq_ref, gk_ref, cos_ref, sin_ref,
    q_ref, kv_ref, rows_ref, weight_ref, total_ref, sems,
):
    c = place_ref[3]
    start = pl.multiple_of((c if mine else 1 - c) * BLOCK, BLOCK)
    step = rows_ref.shape[1] // PARTS
    copies = []
    for k in range(PARTS):
        span = pl.ds(k * step, step)
        copies.append(
            (
                pltpu.make_async_copy(rows_hbm.at[:, span], rows_ref.at[:, span], sems.at[2 * k]),
                pltpu.make_async_copy(
                    weight_hbm.at[span], weight_ref.at[span], sems.at[2 * k + 1]
                ),
            )
        )
    for pair in copies[:2]:
        for copy in pair:
            copy.start()
    for k, pair in enumerate(copies):
        for copy in pair:
            copy.wait()
        if k + 2 < PARTS:
            for copy in copies[k + 2]:
                copy.start()
        span = slice(k * step, (k + 1) * step)
        part = jnp.dot(
            rows_ref[:, span], weight_ref[span, :], preferred_element_type=jnp.float32
        )
        if k == 0:
            total_ref[...] = part
        else:
            total_ref[...] += part
    cosine, sine = cos_ref[pl.ds(start, BLOCK), :], sin_ref[pl.ds(start, BLOCK), :]
    heads = [total_ref[:, h * HEAD_SIZE : (h + 1) * HEAD_SIZE] for h in range(4)]
    kv_ref[0] = head_norm_rope(heads[2], gk_ref[...], cosine, sine).astype(jnp.bfloat16)
    kv_ref[1] = heads[3].astype(jnp.bfloat16)
    for h in range(2):
        q_ref[h] = head_norm_rope(heads[h], gq_ref[...], cosine, sine).astype(jnp.bfloat16)


def whole(shape):
    return pl.BlockSpec(shape, lambda i, p: (0,) * len(shape))


SMEM = pl.BlockSpec(memory_space=pltpu.SMEM)
HBM = pl.BlockSpec(memory_space=pltpu.HBM)
HELD = pl.BlockSpec(memory_space=pltpu.VMEM)


def project(mine, place, rows, weights, tables, name):
    width = weights.shape[0]
    head = jax.ShapeDtypeStruct((2, BLOCK, HEAD_SIZE), jnp.bfloat16)
    return pl.pallas_call(
        functools.partial(project_body, mine),
        in_specs=[SMEM, HBM, HBM] + [HELD] * 4,
        out_specs=[HELD] * 2,
        out_shape=[head] * 2,
        scratch_shapes=[
            pltpu.VMEM((BLOCK, width), jnp.bfloat16),
            pltpu.VMEM((width, 512), jnp.bfloat16),
            pltpu.VMEM((BLOCK, 512), jnp.float32),
            pltpu.SemaphoreType.DMA((2 * PARTS,)),
        ],
        compiler_params=pltpu.CompilerParams(vmem_limit_bytes=60 * MIB),
        cost_estimate=pl.CostEstimate(
            flops=2 * BLOCK * width * 512, bytes_accessed=12 * MIB, transcendentals=0
        ),
        name=name,
    )(place, rows, weights, *tables)


def rows_body(place_ref, *refs):
    pieces, out_ref = refs[:5], refs[5]
    x = place_ref[0]
    quarter, half = BLOCK // X, BLOCK // X // 2
    plan = [(0, 0, quarter), (1, 0, quarter), (2, 0, half), (2, half, half), (3, 0, quarter)]
    for piece, (rel, shift, size) in zip(pieces, plan):
        at = pl.multiple_of(lax.rem(x + rel, X) * quarter + shift, half)
        out_ref[pl.ds(at, size), :] = piece[...]


def place_rows(place, pieces):
    width = pieces[0].shape[1]
    step = 768
    return pl.pallas_call(
        rows_body,
        grid_spec=pltpu.PrefetchScalarGridSpec(
            num_scalar_prefetch=1,
            grid=(width // step,),
            in_specs=[pl.BlockSpec((p.shape[0], step), lambda i, p: (0, i)) for p in pieces],
            out_specs=pl.BlockSpec((BLOCK, step), lambda i, p: (0, i)),
        ),
        out_shape=jax.ShapeDtypeStruct((BLOCK, width), jnp.bfloat16),
        cost_estimate=pl.CostEstimate(flops=0, bytes_accessed=11 * MIB, transcendentals=0),
        name="place_rows",
    )(place, *pieces)


TILE = 256
SPAN = PAIR + TILE


def attend_body(
    place_ref, qmine_ref, qother_ref, mine_ref, other_ref, pmine_ref, pother_ref,
    qoff_ref, koff_ref, keep_ref, give_ref, keys_ref, values_ref,
):
    c = place_ref[3]
    for base, refs in ((0, (pmine_ref, pother_ref)), (PAIR, (mine_ref, other_ref))):
        for block, ref in ((c, refs[0]), (1 - c, refs[1])):
            at = pl.multiple_of(base + block * BLOCK, BLOCK)
            keys_ref[pl.ds(at, BLOCK), :] = ref[0]
            values_ref[pl.ds(at, BLOCK), :] = ref[1]
    for block, q_ref, out_ref in ((1 - c, qother_ref, give_ref), (c, qmine_ref, keep_ref)):
        for tile in range(BLOCK // TILE):
            first, last = tile * TILE, (tile + 1) * TILE
            at = pl.multiple_of(block * BLOCK + first, TILE)
            keys = keys_ref[pl.ds(at, SPAN), :]
            values = values_ref[pl.ds(at, SPAN), :]
            gap = (
                qoff_ref[pl.ds(at, TILE), :]
                - koff_ref[pl.ds(block * (BLOCK // TILE) + tile, 1), :]
            )
            allowed = (gap >= 0) & (gap < LOOKBACK_WINDOW)
            for h in range(2):
                scores = lax.dot_general(
                    q_ref[h, first:last],
                    keys,
                    (((1,), (1,)), ((), ())),
                    preferred_element_type=jnp.float32,
                ) * QS ** (-0.5)
                scores = jnp.where(allowed, scores, -1e30)
                row_max = jnp.max(scores, axis=-1, keepdims=True)
                weights = jnp.exp(scores - row_max)
                totals = jnp.sum(weights, axis=-1, keepdims=True)
                mixed = jnp.dot(
                    weights.astype(jnp.bfloat16), values, preferred_element_type=jnp.float32
                )
                out_ref[first:last, h * HEAD_SIZE : (h + 1) * HEAD_SIZE] = (
                    mixed / totals
                ).astype(jnp.bfloat16)


def attend(place, queries, blocks, query_offsets, key_offsets):
    out = jax.ShapeDtypeStruct((BLOCK, 2 * HEAD_SIZE), jnp.bfloat16)
    return pl.pallas_call(
        attend_body,
        in_specs=[SMEM] + [HELD] * 8,
        out_specs=[HELD] * 2,
        out_shape=[out] * 2,
        scratch_shapes=[pltpu.VMEM((2 * PAIR, HEAD_SIZE), jnp.bfloat16)] * 2,
        compiler_params=pltpu.CompilerParams(vmem_limit_bytes=32 * MIB),
        cost_estimate=pl.CostEstimate(
            flops=4 * PAIR * SPAN * 256, bytes_accessed=3 * MIB, transcendentals=2 * PAIR * SPAN
        ),
        name="attend",
    )(place, *queries, *blocks, query_offsets, key_offsets)


def out_body(place_ref, *refs):
    pieces, (own_ref, other_ref, *outs) = refs[:X], refs[X:]
    rows_ref = outs[X]
    x = place_ref[0]
    quarter = BLOCK // X
    count = own_ref.shape[0] // X
    weights = jnp.concatenate(
        [
            ref[pl.ds(pl.multiple_of(lax.rem(x + k, X) * count, 16), count), :]
            for k in range(X)
            for ref in (own_ref, other_ref)
        ],
        axis=1,
    )
    for k, piece in enumerate(pieces):
        for side in range(2):
            slot = (2 * k + side) * 256
            for rel in range(X):
                at = pl.multiple_of(lax.rem(x + rel, X) * quarter, quarter)
                rows_ref[rel * quarter : (rel + 1) * quarter, slot : slot + 256] = piece[
                    side, pl.ds(at, quarter), :
                ]
    total = lax.dot_general(
        rows_ref[...], weights, (((1,), (1,)), ((), ())), preferred_element_type=jnp.float32
    )
    for rel, out_ref in enumerate(outs[:X]):
        out_ref[...] = total[rel * quarter : (rel + 1) * quarter].astype(jnp.bfloat16)


def out_project(place, pieces, own, other):
    count = own.shape[0] // X
    chunk = jax.ShapeDtypeStruct((BLOCK // X, count), jnp.bfloat16)
    return pl.pallas_call(
        out_body,
        in_specs=[SMEM] + [HELD] * (X + 2),
        out_specs=[HELD] * X,
        out_shape=[chunk] * X,
        scratch_shapes=[
            pltpu.VMEM((BLOCK, 2048), jnp.bfloat16),
        ],
        compiler_params=pltpu.CompilerParams(vmem_limit_bytes=28 * MIB),
        cost_estimate=pl.CostEstimate(
            flops=2 * BLOCK * count * 2048, bytes_accessed=9 * MIB, transcendentals=0
        ),
        name="out_project",
    )(place, *pieces, own, other)


def final_body(place_ref, *refs):
    pieces, (rows_ref, gain_ref, out_ref, stage_ref) = refs[:X], refs[X:]
    x = place_ref[0]
    for k, piece in enumerate(pieces):
        stage_ref[lax.rem(x + k, X)] = piece[...]
    step = 32
    for at in range(0, rows_ref.shape[0], step):
        summed = jnp.concatenate(
            [stage_ref[k, at : at + step].astype(jnp.float32) for k in range(X)], axis=1
        )
        scale = lax.rsqrt(jnp.mean(summed * summed, axis=-1, keepdims=True) + EPSILON)
        out = rows_ref[at : at + step].astype(jnp.float32) + summed * scale * gain_ref[...]
        out_ref[at : at + step] = out.astype(jnp.bfloat16)


def final_norm(place, pieces, rows, gain):
    width = rows.shape[1]
    return pl.pallas_call(
        final_body,
        in_specs=[SMEM] + [HELD] * (X + 2),
        out_specs=HELD,
        out_shape=jax.ShapeDtypeStruct(rows.shape, jnp.bfloat16),
        scratch_shapes=[pltpu.VMEM((X, rows.shape[0], width // X), jnp.bfloat16)],
        compiler_params=pltpu.CompilerParams(vmem_limit_bytes=32 * MIB),
        name="final_norm",
    )(place, *pieces, rows, gain.reshape(1, width))


def core_order(first, second, c):
    low = jnp.where(c == 0, first, second)
    high = jnp.where(c == 0, second, first)
    return low, high


def shards(
    tokens,
    positions,
    w_query,
    key_matrix,
    value_matrix,
    w_out,
    gain_in,
    gain_query,
    gain_key,
    gain_post,
):
    ctx = lax.axis_index("ctx")
    c, y, z, pair = ctx % C, ctx // C % Y, ctx // (Y * C), ctx // C
    x = lax.axis_index("tp")
    place = jnp.stack([x, y, z, c]).astype(jnp.int32)
    width = tokens.shape[1]

    out_rows = w_out.T
    sides = [
        jnp.concatenate(
            [
                w_query[:, side * 256 : side * 256 + 256],
                key_matrix[:, side * 128 : side * 128 + 128],
                value_matrix[:, side * 128 : side * 128 + 128],
                out_rows[:, side * 256 : side * 256 + 256],
            ],
            axis=1,
        )
        for side in range(2)
    ]
    mine, theirs = core_order(sides[0], sides[1], c)
    received = swap_cores(theirs)
    stacked = jnp.concatenate(core_order(mine, received, c), axis=0)
    part, part_out = stacked[:, :512], trade_x_z(stacked[:, 512:])
    part = lax.all_gather(part, "ctx", axis=0, tiled=True, axis_index_groups=ROWS)
    part, moving = together(part, tokens)
    weights = lax.all_gather(part, "ctx", axis=0, tiled=True, axis_index_groups=COLUMNS)

    start = pair * PAIR
    query_offsets = lax.dynamic_slice_in_dim(positions, start, PAIR, 0) - positions[0]
    before = lax.dynamic_slice_in_dim(positions, jnp.maximum(start - PAIR, 0), PAIR, 0)
    before = jnp.where(pair == 0, -(2**30), before - positions[0])
    key_offsets = jnp.concatenate([before, query_offsets])
    key_offsets = jnp.stack([key_offsets[at : at + SPAN] for at in range(0, PAIR, TILE)])
    half_dim = HEAD_SIZE // 2
    frequency = ROPE_BASE ** (-(jnp.arange(half_dim, dtype=jnp.float32) * 2.0) / HEAD_SIZE)
    angles = query_offsets.astype(jnp.float32)[:, None] * frequency[None, :]
    cosine, sine = jnp.cos(angles), jnp.sin(angles)
    cosine = jnp.concatenate([cosine, cosine], axis=1)
    sine = jnp.concatenate([-sine, sine], axis=1)
    query_offsets = query_offsets[:, None]

    rows = input_norm(moving, gain_in)
    from_low, from_high = shift_x(rows, 1), shift_x(rows, -1)
    part_out = lax.all_gather(part_out, "ctx", axis=0, tiled=True, axis_index_groups=ROWS)
    from_low, from_high, part_out, cosine, sine, query_offsets, key_offsets = together(
        from_low, from_high, part_out, cosine, sine, query_offsets, key_offsets
    )
    half = rows.shape[0] // 2
    far_low = shift_x(from_low[:half], 1)
    far_high = shift_x(from_high[half:], -1)
    own_rows = place_rows(place, [rows, from_high, far_low, far_high, from_low])
    other_rows = swap_cores(own_rows)

    tables = [gain_query.reshape(1, HEAD_SIZE), gain_key.reshape(1, HEAD_SIZE), cosine, sine]

    weights, part_out = together(weights, part_out)
    own_out = lax.all_gather(part_out, "ctx", axis=0, tiled=True, axis_index_groups=COLUMNS)
    q_own, kv_own = project(True, place, own_rows, weights, tables, "project_own")
    prev_own = next_pair(kv_own)
    q_other, kv_other = project(False, place, other_rows, weights, tables, "project_other")
    prev_other = next_pair(kv_other)
    blocks = [kv_own, kv_other, prev_own, prev_other]
    keep, give = attend(place, [q_own, q_other], blocks, query_offsets, key_offsets)
    other = swap_cores(give)
    other, own_out = together(other, own_out)
    both = jnp.stack([keep, other])
    attended = [both, shift_x(both, -1), shift_x(both, 2), shift_x(both, 1)]
    other_out = swap_cores(own_out)
    sums = out_project(place, attended, own_out, other_out)
    sums = [sums[0], shift_x(sums[3], -1), shift_x(sums[2], 2), shift_x(sums[1], 1)]
    return final_norm(place, sums, tokens, gain_post)


def solution(mesh):
    in_specs = (
        P(("ctx", "tp"), None),
        P(),
        P("ctx", "tp"),
        P("ctx", "tp"),
        P("ctx", "tp"),
        P("tp", "ctx"),
        P(),
        P(),
        P(),
        P(),
    )
    out_specs = P(("ctx", "tp"), None)
    return jax.shard_map(shards, mesh=mesh, in_specs=in_specs, out_specs=out_specs, check_vma=False)
```

```python
import functools

import jax
import jax.numpy as jnp
from jax import lax
from jax.experimental import pallas as pl
from jax.experimental.pallas import tpu as pltpu
from jax.sharding import PartitionSpec as P

HEAD_SIZE = 128
QS = 168
LOOKBACK_WINDOW = 1024
EPSILON = 1e-06
ROPE_BASE = 10000.0
Z, Y, C, X = 8, 4, 2, 4
BLOCK = 512
PAIR = 1024
VMEM = pltpu.VMEM
MIB = 1024 * 1024


def ctx_pairs(move):
    pairs = []
    for source in range(Z * Y * C):
        target = move(source // (Y * C), source // C % Y, source % C)
        if target is not None:
            z, y, c = target
            pairs.append((source, (z % Z) * Y * C + (y % Y) * C + c))
    return pairs


def swap_cores(value):
    return lax.ppermute(value, "ctx", ctx_pairs(lambda z, y, c: (z, y, 1 - c)))


def shift_x(value, steps):
    return lax.ppermute(value, "tp", [(x, (x + steps) % X) for x in range(X)])


def next_pair(value):
    pairs = [(source, source + C) for source in range(Z * Y * C - C)]
    return lax.ppermute(value, "ctx", pairs)


def shift_y(value, steps):
    return lax.ppermute(value, "ctx", ctx_pairs(lambda z, y, c: (z, y + steps, c)))


def shift_z(value, steps):
    return lax.ppermute(value, "ctx", ctx_pairs(lambda z, y, c: (z + steps, y, c)))


def trade_x_z(value):
    pairs = []
    for source in range(Z * Y * C * X):
        ctx, x = source // X, source % X
        z, rest = ctx // (Y * C), ctx % (Y * C)
        pairs.append((source, ((x * 2 + z % 2) * Y * C + rest) * X + z // 2))
    return lax.ppermute(value, ("ctx", "tp"), pairs)


def together(*values):
    return lax.optimization_barrier(values)


ROWS = [[z * Y * C + y * C + c for y in range(Y)] for z in range(Z) for c in range(C)]
COLUMNS = [[z * Y * C + y * C + c for z in range(Z)] for y in range(Y) for c in range(C)]


def norm_body(rows_ref, gain_ref, out_ref):
    rows = rows_ref[...].astype(jnp.float32)
    scale = lax.rsqrt(jnp.mean(rows * rows, axis=-1, keepdims=True) + EPSILON)
    out_ref[...] = (rows * scale * gain_ref[...]).astype(jnp.bfloat16)


def input_norm(rows, gain):
    count, width = rows.shape
    step = 32
    return pl.pallas_call(
        norm_body,
        grid=(count // step,),
        in_specs=[
            pl.BlockSpec((step, width), lambda i: (i, 0)),
            pl.BlockSpec((1, width), lambda i: (0, 0)),
        ],
        out_specs=pl.BlockSpec((step, width), lambda i: (i, 0)),
        out_shape=jax.ShapeDtypeStruct(rows.shape, jnp.bfloat16),
        name="input_norm",
    )(rows, gain.reshape(1, width))


def head_norm_rope(raw, gain, cosine, sine):
    scale = lax.rsqrt(jnp.mean(raw * raw, axis=-1, keepdims=True) + EPSILON)
    normed = raw * scale * gain
    return normed * cosine + pltpu.roll(normed, HEAD_SIZE // 2, 1) * sine


PARTS = 3


def project_body(
    mine, place_ref, rows_hbm, weight_ref, gq_ref, gk_ref, cos_ref, sin_ref,
    q_ref, kv_ref, rows_ref, total_ref, sems,
):
    c = place_ref[3]
    start = pl.multiple_of((c if mine else 1 - c) * BLOCK, BLOCK)
    step = rows_ref.shape[1] // PARTS
    copies = []
    for k in range(PARTS):
        span = pl.ds(k * step, step)
        copies.append(
            pltpu.make_async_copy(rows_hbm.at[:, span], rows_ref.at[:, span], sems.at[k])
        )
    for copy in copies:
        copy.start()
    for k, copy in enumerate(copies):
        copy.wait()
        span = slice(k * step, (k + 1) * step)
        part = jnp.dot(
            rows_ref[:, span], weight_ref[span, :], preferred_element_type=jnp.float32
        )
        if k == 0:
            total_ref[...] = part
        else:
            total_ref[...] += part
    cosine, sine = cos_ref[pl.ds(start, BLOCK), :], sin_ref[pl.ds(start, BLOCK), :]
    heads = [total_ref[:, h * HEAD_SIZE : (h + 1) * HEAD_SIZE] for h in range(4)]
    kv_ref[0] = head_norm_rope(heads[2], gk_ref[...], cosine, sine).astype(jnp.bfloat16)
    kv_ref[1] = heads[3].astype(jnp.bfloat16)
    for h in range(2):
        q_ref[h] = head_norm_rope(heads[h], gq_ref[...], cosine, sine).astype(jnp.bfloat16)


def whole(shape):
    return pl.BlockSpec(shape, lambda i, p: (0,) * len(shape))


SMEM = pl.BlockSpec(memory_space=pltpu.SMEM)
HBM = pl.BlockSpec(memory_space=pltpu.HBM)
HELD = pl.BlockSpec(memory_space=pltpu.VMEM)


def project(mine, place, rows, weights, tables, name):
    width = weights.shape[0]
    head = jax.ShapeDtypeStruct((2, BLOCK, HEAD_SIZE), jnp.bfloat16)
    return pl.pallas_call(
        functools.partial(project_body, mine),
        in_specs=[SMEM, HBM] + [HELD] * 5,
        out_specs=[HELD] * 2,
        out_shape=[head] * 2,
        scratch_shapes=[
            pltpu.VMEM((BLOCK, width), jnp.bfloat16),
            pltpu.VMEM((BLOCK, 512), jnp.float32),
            pltpu.SemaphoreType.DMA((PARTS,)),
        ],
        compiler_params=pltpu.CompilerParams(vmem_limit_bytes=50 * MIB),
        cost_estimate=pl.CostEstimate(
            flops=2 * BLOCK * width * 512, bytes_accessed=12 * MIB, transcendentals=0
        ),
        name=name,
    )(place, rows, weights, *tables)


def rows_body(place_ref, *refs):
    pieces, out_ref = refs[:5], refs[5]
    x = place_ref[0]
    quarter, half = BLOCK // X, BLOCK // X // 2
    plan = [(0, 0, quarter), (1, 0, quarter), (2, 0, half), (2, half, half), (3, 0, quarter)]
    for piece, (rel, shift, size) in zip(pieces, plan):
        at = pl.multiple_of(lax.rem(x + rel, X) * quarter + shift, half)
        out_ref[pl.ds(at, size), :] = piece[...]


def place_rows(place, pieces):
    width = pieces[0].shape[1]
    step = 768
    return pl.pallas_call(
        rows_body,
        grid_spec=pltpu.PrefetchScalarGridSpec(
            num_scalar_prefetch=1,
            grid=(width // step,),
            in_specs=[pl.BlockSpec((p.shape[0], step), lambda i, p: (0, i)) for p in pieces],
            out_specs=pl.BlockSpec((BLOCK, step), lambda i, p: (0, i)),
        ),
        out_shape=jax.ShapeDtypeStruct((BLOCK, width), jnp.bfloat16),
        cost_estimate=pl.CostEstimate(flops=0, bytes_accessed=11 * MIB, transcendentals=0),
        name="place_rows",
    )(place, *pieces)


TILE = 256
SPAN = PAIR + TILE


def attend_body(
    place_ref, qmine_ref, qother_ref, mine_ref, other_ref, pmine_ref, pother_ref,
    qoff_ref, koff_ref, keep_ref, give_ref, keys_ref, values_ref,
):
    c = place_ref[3]
    for base, refs in ((0, (pmine_ref, pother_ref)), (PAIR, (mine_ref, other_ref))):
        for block, ref in ((c, refs[0]), (1 - c, refs[1])):
            at = pl.multiple_of(base + block * BLOCK, BLOCK)
            keys_ref[pl.ds(at, BLOCK), :] = ref[0]
            values_ref[pl.ds(at, BLOCK), :] = ref[1]
    for block, q_ref, out_ref in ((1 - c, qother_ref, give_ref), (c, qmine_ref, keep_ref)):
        for tile in range(BLOCK // TILE):
            first, last = tile * TILE, (tile + 1) * TILE
            at = pl.multiple_of(block * BLOCK + first, TILE)
            keys = keys_ref[pl.ds(at, SPAN), :]
            values = values_ref[pl.ds(at, SPAN), :]
            gap = (
                qoff_ref[pl.ds(at, TILE), :]
                - koff_ref[pl.ds(block * (BLOCK // TILE) + tile, 1), :]
            )
            allowed = (gap >= 0) & (gap < LOOKBACK_WINDOW)
            for h in range(2):
                scores = lax.dot_general(
                    q_ref[h, first:last],
                    keys,
                    (((1,), (1,)), ((), ())),
                    preferred_element_type=jnp.float32,
                ) * QS ** (-0.5)
                scores = jnp.where(allowed, scores, -1e30)
                row_max = jnp.max(scores, axis=-1, keepdims=True)
                weights = jnp.exp(scores - row_max)
                totals = jnp.sum(weights, axis=-1, keepdims=True)
                mixed = jnp.dot(
                    weights.astype(jnp.bfloat16), values, preferred_element_type=jnp.float32
                )
                out_ref[first:last, h * HEAD_SIZE : (h + 1) * HEAD_SIZE] = (
                    mixed / totals
                ).astype(jnp.bfloat16)


def attend(place, queries, blocks, query_offsets, key_offsets):
    out = jax.ShapeDtypeStruct((BLOCK, 2 * HEAD_SIZE), jnp.bfloat16)
    return pl.pallas_call(
        attend_body,
        in_specs=[SMEM] + [HELD] * 8,
        out_specs=[HELD] * 2,
        out_shape=[out] * 2,
        scratch_shapes=[pltpu.VMEM((2 * PAIR, HEAD_SIZE), jnp.bfloat16)] * 2,
        compiler_params=pltpu.CompilerParams(vmem_limit_bytes=32 * MIB),
        cost_estimate=pl.CostEstimate(
            flops=4 * PAIR * SPAN * 256, bytes_accessed=3 * MIB, transcendentals=2 * PAIR * SPAN
        ),
        name="attend",
    )(place, *queries, *blocks, query_offsets, key_offsets)


def out_body(place_ref, *refs):
    pieces, (own_ref, other_ref, *outs) = refs[:X], refs[X:]
    rows_ref = outs[X]
    x = place_ref[0]
    quarter = BLOCK // X
    count = own_ref.shape[0] // X
    weights = jnp.concatenate(
        [
            ref[pl.ds(pl.multiple_of(lax.rem(x + k, X) * count, 16), count), :]
            for k in range(X)
            for ref in (own_ref, other_ref)
        ],
        axis=1,
    )
    for k, piece in enumerate(pieces):
        for side in range(2):
            slot = (2 * k + side) * 256
            for rel in range(X):
                at = pl.multiple_of(lax.rem(x + rel, X) * quarter, quarter)
                rows_ref[rel * quarter : (rel + 1) * quarter, slot : slot + 256] = piece[
                    side, pl.ds(at, quarter), :
                ]
    total = lax.dot_general(
        rows_ref[...], weights, (((1,), (1,)), ((), ())), preferred_element_type=jnp.float32
    )
    for rel, out_ref in enumerate(outs[:X]):
        out_ref[...] = total[rel * quarter : (rel + 1) * quarter].astype(jnp.bfloat16)


def out_project(place, pieces, own, other):
    count = own.shape[0] // X
    chunk = jax.ShapeDtypeStruct((BLOCK // X, count), jnp.bfloat16)
    return pl.pallas_call(
        out_body,
        in_specs=[SMEM] + [HELD] * (X + 2),
        out_specs=[HELD] * X,
        out_shape=[chunk] * X,
        scratch_shapes=[
            pltpu.VMEM((BLOCK, 2048), jnp.bfloat16),
        ],
        compiler_params=pltpu.CompilerParams(vmem_limit_bytes=28 * MIB),
        cost_estimate=pl.CostEstimate(
            flops=2 * BLOCK * count * 2048, bytes_accessed=9 * MIB, transcendentals=0
        ),
        name="out_project",
    )(place, *pieces, own, other)


def final_body(place_ref, *refs):
    pieces, (rows_ref, gain_ref, out_ref, stage_ref) = refs[:X], refs[X:]
    x = place_ref[0]
    for k, piece in enumerate(pieces):
        stage_ref[lax.rem(x + k, X)] = piece[...]
    step = 32
    for at in range(0, rows_ref.shape[0], step):
        summed = jnp.concatenate(
            [stage_ref[k, at : at + step].astype(jnp.float32) for k in range(X)], axis=1
        )
        scale = lax.rsqrt(jnp.mean(summed * summed, axis=-1, keepdims=True) + EPSILON)
        out = rows_ref[at : at + step].astype(jnp.float32) + summed * scale * gain_ref[...]
        out_ref[at : at + step] = out.astype(jnp.bfloat16)


def final_norm(place, pieces, rows, gain):
    width = rows.shape[1]
    return pl.pallas_call(
        final_body,
        in_specs=[SMEM] + [HELD] * (X + 2),
        out_specs=HELD,
        out_shape=jax.ShapeDtypeStruct(rows.shape, jnp.bfloat16),
        scratch_shapes=[pltpu.VMEM((X, rows.shape[0], width // X), jnp.bfloat16)],
        compiler_params=pltpu.CompilerParams(vmem_limit_bytes=32 * MIB),
        name="final_norm",
    )(place, *pieces, rows, gain.reshape(1, width))


def core_order(first, second, c):
    low = jnp.where(c == 0, first, second)
    high = jnp.where(c == 0, second, first)
    return low, high


def shards(
    tokens,
    positions,
    w_query,
    key_matrix,
    value_matrix,
    w_out,
    gain_in,
    gain_query,
    gain_key,
    gain_post,
):
    ctx = lax.axis_index("ctx")
    c, y, z, pair = ctx % C, ctx // C % Y, ctx // (Y * C), ctx // C
    x = lax.axis_index("tp")
    place = jnp.stack([x, y, z, c]).astype(jnp.int32)
    width = tokens.shape[1]

    out_rows = w_out.T
    sides = [
        jnp.concatenate(
            [
                w_query[:, side * 256 : side * 256 + 256],
                key_matrix[:, side * 128 : side * 128 + 128],
                value_matrix[:, side * 128 : side * 128 + 128],
                out_rows[:, side * 256 : side * 256 + 256],
            ],
            axis=1,
        )
        for side in range(2)
    ]
    mine, theirs = core_order(sides[0], sides[1], c)
    received = swap_cores(theirs)
    stacked = jnp.concatenate(core_order(mine, received, c), axis=0)
    part, part_out = stacked[:, :512], trade_x_z(stacked[:, 512:])
    part = lax.all_gather(part, "ctx", axis=0, tiled=True, axis_index_groups=ROWS)
    part, moving = together(part, tokens)
    weights = lax.all_gather(part, "ctx", axis=0, tiled=True, axis_index_groups=COLUMNS)

    start = pair * PAIR
    query_offsets = lax.dynamic_slice_in_dim(positions, start, PAIR, 0) - positions[0]
    before = lax.dynamic_slice_in_dim(positions, jnp.maximum(start - PAIR, 0), PAIR, 0)
    before = jnp.where(pair == 0, -(2**30), before - positions[0])
    key_offsets = jnp.concatenate([before, query_offsets])
    key_offsets = jnp.stack([key_offsets[at : at + SPAN] for at in range(0, PAIR, TILE)])
    half_dim = HEAD_SIZE // 2
    frequency = ROPE_BASE ** (-(jnp.arange(half_dim, dtype=jnp.float32) * 2.0) / HEAD_SIZE)
    angles = query_offsets.astype(jnp.float32)[:, None] * frequency[None, :]
    cosine, sine = jnp.cos(angles), jnp.sin(angles)
    cosine = jnp.concatenate([cosine, cosine], axis=1)
    sine = jnp.concatenate([-sine, sine], axis=1)
    query_offsets = query_offsets[:, None]

    rows = input_norm(moving, gain_in)
    from_low, from_high = shift_x(rows, 1), shift_x(rows, -1)
    part_out = lax.all_gather(part_out, "ctx", axis=0, tiled=True, axis_index_groups=ROWS)
    from_low, from_high, part_out, cosine, sine, query_offsets, key_offsets = together(
        from_low, from_high, part_out, cosine, sine, query_offsets, key_offsets
    )
    half = rows.shape[0] // 2
    far_low = shift_x(from_low[:half], 1)
    far_high = shift_x(from_high[half:], -1)
    own_rows = place_rows(place, [rows, from_high, far_low, far_high, from_low])
    other_rows = swap_cores(own_rows)

    tables = [gain_query.reshape(1, HEAD_SIZE), gain_key.reshape(1, HEAD_SIZE), cosine, sine]

    weights, part_out = together(weights, part_out)
    own_out = lax.all_gather(part_out, "ctx", axis=0, tiled=True, axis_index_groups=COLUMNS)
    q_own, kv_own = project(True, place, own_rows, weights, tables, "project_own")
    prev_own = next_pair(kv_own)
    q_other, kv_other = project(False, place, other_rows, weights, tables, "project_other")
    prev_other = next_pair(kv_other)
    blocks = [kv_own, kv_other, prev_own, prev_other]
    keep, give = attend(place, [q_own, q_other], blocks, query_offsets, key_offsets)
    other = swap_cores(give)
    other, own_out = together(other, own_out)
    both = jnp.stack([keep, other])
    attended = [both, shift_x(both, -1), shift_x(both, 2), shift_x(both, 1)]
    other_out = swap_cores(own_out)
    sums = out_project(place, attended, own_out, other_out)
    sums = [sums[0], shift_x(sums[3], -1), shift_x(sums[2], 2), shift_x(sums[1], 1)]
    return final_norm(place, sums, tokens, gain_post)


def solution(mesh):
    in_specs = (
        P(("ctx", "tp"), None),
        P(),
        P("ctx", "tp"),
        P("ctx", "tp"),
        P("ctx", "tp"),
        P("tp", "ctx"),
        P(),
        P(),
        P(),
        P(),
    )
    out_specs = P(("ctx", "tp"), None)
    return jax.shard_map(shards, mesh=mesh, in_specs=in_specs, out_specs=out_specs, check_vma=False)
```

```python
import functools

import jax
import jax.numpy as jnp
from jax import lax
from jax.experimental import pallas as pl
from jax.experimental.pallas import tpu as pltpu
from jax.sharding import PartitionSpec as P

HEAD_SIZE = 128
QS = 168
LOOKBACK_WINDOW = 1024
EPSILON = 1e-06
ROPE_BASE = 10000.0
Z, Y, C, X = 8, 4, 2, 4
BLOCK = 512
PAIR = 1024
VMEM = pltpu.VMEM
MIB = 1024 * 1024


def ctx_pairs(move):
    pairs = []
    for source in range(Z * Y * C):
        target = move(source // (Y * C), source // C % Y, source % C)
        if target is not None:
            z, y, c = target
            pairs.append((source, (z % Z) * Y * C + (y % Y) * C + c))
    return pairs


def swap_cores(value):
    return lax.ppermute(value, "ctx", ctx_pairs(lambda z, y, c: (z, y, 1 - c)))


def shift_x(value, steps):
    return lax.ppermute(value, "tp", [(x, (x + steps) % X) for x in range(X)])


def next_pair(value):
    pairs = [(source, source + C) for source in range(Z * Y * C - C)]
    return lax.ppermute(value, "ctx", pairs)


def shift_y(value, steps):
    return lax.ppermute(value, "ctx", ctx_pairs(lambda z, y, c: (z, y + steps, c)))


def shift_z(value, steps):
    return lax.ppermute(value, "ctx", ctx_pairs(lambda z, y, c: (z + steps, y, c)))


def trade_x_z(value):
    pairs = []
    for source in range(Z * Y * C * X):
        ctx, x = source // X, source % X
        z, rest = ctx // (Y * C), ctx % (Y * C)
        pairs.append((source, ((x * 2 + z % 2) * Y * C + rest) * X + z // 2))
    return lax.ppermute(value, ("ctx", "tp"), pairs)


def together(*values):
    return lax.optimization_barrier(values)


ROWS = [[z * Y * C + y * C + c for y in range(Y)] for z in range(Z) for c in range(C)]
COLUMNS = [[z * Y * C + y * C + c for z in range(Z)] for y in range(Y) for c in range(C)]


def norm_body(rows_ref, gain_ref, out_ref):
    rows = rows_ref[...].astype(jnp.float32)
    scale = lax.rsqrt(jnp.mean(rows * rows, axis=-1, keepdims=True) + EPSILON)
    out_ref[...] = (rows * scale * gain_ref[...]).astype(jnp.bfloat16)


def input_norm(rows, gain):
    count, width = rows.shape
    step = 32
    return pl.pallas_call(
        norm_body,
        grid=(count // step,),
        in_specs=[
            pl.BlockSpec((step, width), lambda i: (i, 0)),
            pl.BlockSpec((1, width), lambda i: (0, 0)),
        ],
        out_specs=pl.BlockSpec((step, width), lambda i: (i, 0)),
        out_shape=jax.ShapeDtypeStruct(rows.shape, jnp.bfloat16),
        name="input_norm",
    )(rows, gain.reshape(1, width))


def head_norm_rope(raw, gain, cosine, sine):
    scale = lax.rsqrt(jnp.mean(raw * raw, axis=-1, keepdims=True) + EPSILON)
    normed = raw * scale * gain
    return normed * cosine + pltpu.roll(normed, HEAD_SIZE // 2, 1) * sine


PARTS = 3


def project_body(
    mine, place_ref, rows_hbm, weight_ref, gq_ref, gk_ref, cos_ref, sin_ref,
    q_ref, kv_ref, rows_ref, total_ref, sems,
):
    c = place_ref[3]
    start = pl.multiple_of((c if mine else 1 - c) * BLOCK, BLOCK)
    step = rows_ref.shape[1] // PARTS
    copies = []
    for k in range(PARTS):
        span = pl.ds(k * step, step)
        copies.append(
            pltpu.make_async_copy(rows_hbm.at[:, span], rows_ref.at[:, span], sems.at[k])
        )
    for copy in copies:
        copy.start()
    for k, copy in enumerate(copies):
        copy.wait()
        span = slice(k * step, (k + 1) * step)
        part = jnp.dot(
            rows_ref[:, span], weight_ref[span, :], preferred_element_type=jnp.float32
        )
        if k == 0:
            total_ref[...] = part
        else:
            total_ref[...] += part
    cosine, sine = cos_ref[pl.ds(start, BLOCK), :], sin_ref[pl.ds(start, BLOCK), :]
    heads = [total_ref[:, h * HEAD_SIZE : (h + 1) * HEAD_SIZE] for h in range(4)]
    kv_ref[0] = head_norm_rope(heads[2], gk_ref[...], cosine, sine).astype(jnp.bfloat16)
    kv_ref[1] = heads[3].astype(jnp.bfloat16)
    for h in range(2):
        q_ref[h] = head_norm_rope(heads[h], gq_ref[...], cosine, sine).astype(jnp.bfloat16)


def whole(shape):
    return pl.BlockSpec(shape, lambda i, p: (0,) * len(shape))


SMEM = pl.BlockSpec(memory_space=pltpu.SMEM)
HBM = pl.BlockSpec(memory_space=pltpu.HBM)
HELD = pl.BlockSpec(memory_space=pltpu.VMEM)


def project(mine, place, rows, weights, tables, name):
    width = weights.shape[0]
    head = jax.ShapeDtypeStruct((2, BLOCK, HEAD_SIZE), jnp.bfloat16)
    return pl.pallas_call(
        functools.partial(project_body, mine),
        in_specs=[SMEM, HBM] + [HELD] * 5,
        out_specs=[HELD] * 2,
        out_shape=[head] * 2,
        scratch_shapes=[
            pltpu.VMEM((BLOCK, width), jnp.bfloat16),
            pltpu.VMEM((BLOCK, 512), jnp.float32),
            pltpu.SemaphoreType.DMA((PARTS,)),
        ],
        compiler_params=pltpu.CompilerParams(vmem_limit_bytes=50 * MIB),
        cost_estimate=pl.CostEstimate(
            flops=2 * BLOCK * width * 512, bytes_accessed=12 * MIB, transcendentals=0
        ),
        name=name,
    )(place, rows, weights, *tables)


def rows_body(place_ref, *refs):
    pieces, out_ref = refs[:5], refs[5]
    x = place_ref[0]
    quarter, half = BLOCK // X, BLOCK // X // 2
    plan = [(0, 0, quarter), (1, 0, quarter), (2, 0, half), (2, half, half), (3, 0, quarter)]
    for piece, (rel, shift, size) in zip(pieces, plan):
        at = pl.multiple_of(lax.rem(x + rel, X) * quarter + shift, half)
        out_ref[pl.ds(at, size), :] = piece[...]


def place_rows(place, pieces):
    width = pieces[0].shape[1]
    step = 768
    return pl.pallas_call(
        rows_body,
        grid_spec=pltpu.PrefetchScalarGridSpec(
            num_scalar_prefetch=1,
            grid=(width // step,),
            in_specs=[pl.BlockSpec((p.shape[0], step), lambda i, p: (0, i)) for p in pieces],
            out_specs=pl.BlockSpec((BLOCK, step), lambda i, p: (0, i)),
        ),
        out_shape=jax.ShapeDtypeStruct((BLOCK, width), jnp.bfloat16),
        cost_estimate=pl.CostEstimate(flops=0, bytes_accessed=11 * MIB, transcendentals=0),
        name="place_rows",
    )(place, *pieces)


TILE = 256
SPAN = PAIR + TILE


def attend_body(
    place_ref, qmine_ref, qother_ref, mine_ref, other_ref, pmine_ref, pother_ref,
    qoff_ref, koff_ref, keep_ref, give_ref, keys_ref, values_ref,
):
    c = place_ref[3]
    for base, refs in ((0, (pmine_ref, pother_ref)), (PAIR, (mine_ref, other_ref))):
        for block, ref in ((c, refs[0]), (1 - c, refs[1])):
            at = pl.multiple_of(base + block * BLOCK, BLOCK)
            keys_ref[pl.ds(at, BLOCK), :] = ref[0]
            values_ref[pl.ds(at, BLOCK), :] = ref[1]
    for block, q_ref, out_ref in ((1 - c, qother_ref, give_ref), (c, qmine_ref, keep_ref)):
        for tile in range(BLOCK // TILE):
            first, last = tile * TILE, (tile + 1) * TILE
            at = pl.multiple_of(block * BLOCK + first, TILE)
            keys = keys_ref[pl.ds(at, SPAN), :]
            values = values_ref[pl.ds(at, SPAN), :]
            gap = (
                qoff_ref[pl.ds(at, TILE), :]
                - koff_ref[pl.ds(block * (BLOCK // TILE) + tile, 1), :]
            )
            allowed = (gap >= 0) & (gap < LOOKBACK_WINDOW)
            for h in range(2):
                scores = lax.dot_general(
                    q_ref[h, first:last],
                    keys,
                    (((1,), (1,)), ((), ())),
                    preferred_element_type=jnp.float32,
                ) * QS ** (-0.5)
                scores = jnp.where(allowed, scores, -1e30)
                row_max = jnp.max(scores, axis=-1, keepdims=True)
                weights = jnp.exp(scores - row_max)
                totals = jnp.sum(weights, axis=-1, keepdims=True)
                mixed = jnp.dot(
                    weights.astype(jnp.bfloat16), values, preferred_element_type=jnp.float32
                )
                out_ref[first:last, h * HEAD_SIZE : (h + 1) * HEAD_SIZE] = (
                    mixed / totals
                ).astype(jnp.bfloat16)


def attend(place, queries, blocks, query_offsets, key_offsets):
    out = jax.ShapeDtypeStruct((BLOCK, 2 * HEAD_SIZE), jnp.bfloat16)
    return pl.pallas_call(
        attend_body,
        in_specs=[SMEM] + [HELD] * 8,
        out_specs=[HELD] * 2,
        out_shape=[out] * 2,
        scratch_shapes=[pltpu.VMEM((2 * PAIR, HEAD_SIZE), jnp.bfloat16)] * 2,
        compiler_params=pltpu.CompilerParams(vmem_limit_bytes=32 * MIB),
        cost_estimate=pl.CostEstimate(
            flops=4 * PAIR * SPAN * 256, bytes_accessed=3 * MIB, transcendentals=2 * PAIR * SPAN
        ),
        name="attend",
    )(place, *queries, *blocks, query_offsets, key_offsets)


def out_body(place_ref, *refs):
    pieces, (own_ref, other_ref, *outs) = refs[:X], refs[X:]
    rows_ref = outs[X]
    x = place_ref[0]
    quarter = BLOCK // X
    count = own_ref.shape[0] // X
    weights = jnp.concatenate(
        [
            ref[pl.ds(pl.multiple_of(lax.rem(x + k, X) * count, 16), count), :]
            for k in range(X)
            for ref in (own_ref, other_ref)
        ],
        axis=1,
    )
    for k, piece in enumerate(pieces):
        for side in range(2):
            slot = (2 * k + side) * 256
            for rel in range(X):
                at = pl.multiple_of(lax.rem(x + rel, X) * quarter, quarter)
                rows_ref[rel * quarter : (rel + 1) * quarter, slot : slot + 256] = piece[
                    side, pl.ds(at, quarter), :
                ]
    total = lax.dot_general(
        rows_ref[...], weights, (((1,), (1,)), ((), ())), preferred_element_type=jnp.float32
    )
    for rel, out_ref in enumerate(outs[:X]):
        out_ref[...] = total[rel * quarter : (rel + 1) * quarter].astype(jnp.bfloat16)


def out_project(place, pieces, own, other):
    count = own.shape[0] // X
    chunk = jax.ShapeDtypeStruct((BLOCK // X, count), jnp.bfloat16)
    return pl.pallas_call(
        out_body,
        in_specs=[SMEM] + [HELD] * (X + 2),
        out_specs=[HELD] * X,
        out_shape=[chunk] * X,
        scratch_shapes=[
            pltpu.VMEM((BLOCK, 2048), jnp.bfloat16),
        ],
        compiler_params=pltpu.CompilerParams(vmem_limit_bytes=28 * MIB),
        cost_estimate=pl.CostEstimate(
            flops=2 * BLOCK * count * 2048, bytes_accessed=9 * MIB, transcendentals=0
        ),
        name="out_project",
    )(place, *pieces, own, other)


def final_body(place_ref, *refs):
    pieces, (rows_ref, gain_ref, out_ref, stage_ref) = refs[:X], refs[X:]
    x = place_ref[0]
    for k, piece in enumerate(pieces):
        stage_ref[lax.rem(x + k, X)] = piece[...]
    step = 32
    for at in range(0, rows_ref.shape[0], step):
        summed = jnp.concatenate(
            [stage_ref[k, at : at + step].astype(jnp.float32) for k in range(X)], axis=1
        )
        scale = lax.rsqrt(jnp.mean(summed * summed, axis=-1, keepdims=True) + EPSILON)
        out = rows_ref[at : at + step].astype(jnp.float32) + summed * scale * gain_ref[...]
        out_ref[at : at + step] = out.astype(jnp.bfloat16)


def final_norm(place, pieces, rows, gain):
    width = rows.shape[1]
    return pl.pallas_call(
        final_body,
        in_specs=[SMEM] + [HELD] * (X + 2),
        out_specs=HELD,
        out_shape=jax.ShapeDtypeStruct(rows.shape, jnp.bfloat16),
        scratch_shapes=[pltpu.VMEM((X, rows.shape[0], width // X), jnp.bfloat16)],
        compiler_params=pltpu.CompilerParams(vmem_limit_bytes=32 * MIB),
        name="final_norm",
    )(place, *pieces, rows, gain.reshape(1, width))


def core_order(first, second, c):
    low = jnp.where(c == 0, first, second)
    high = jnp.where(c == 0, second, first)
    return low, high


def shards(
    tokens,
    positions,
    w_query,
    key_matrix,
    value_matrix,
    w_out,
    gain_in,
    gain_query,
    gain_key,
    gain_post,
):
    ctx = lax.axis_index("ctx")
    c, y, z, pair = ctx % C, ctx // C % Y, ctx // (Y * C), ctx // C
    x = lax.axis_index("tp")
    place = jnp.stack([x, y, z, c]).astype(jnp.int32)
    width = tokens.shape[1]

    out_rows = w_out.T
    sides = [
        jnp.concatenate(
            [
                w_query[:, side * 256 : side * 256 + 256],
                key_matrix[:, side * 128 : side * 128 + 128],
                value_matrix[:, side * 128 : side * 128 + 128],
                out_rows[:, side * 256 : side * 256 + 256],
            ],
            axis=1,
        )
        for side in range(2)
    ]
    mine, theirs = core_order(sides[0], sides[1], c)
    received = swap_cores(theirs)
    stacked = jnp.concatenate(core_order(mine, received, c), axis=0)
    part, part_out = stacked[:, :512], trade_x_z(stacked[:, 512:])
    part = lax.all_gather(part, "ctx", axis=0, tiled=True, axis_index_groups=ROWS)
    part, moving = together(part, tokens)
    weights = lax.all_gather(part, "ctx", axis=0, tiled=True, axis_index_groups=COLUMNS)

    start = pair * PAIR
    query_offsets = lax.dynamic_slice_in_dim(positions, start, PAIR, 0) - positions[0]
    before = lax.dynamic_slice_in_dim(positions, jnp.maximum(start - PAIR, 0), PAIR, 0)
    before = jnp.where(pair == 0, -(2**30), before - positions[0])
    key_offsets = jnp.concatenate([before, query_offsets])
    key_offsets = jnp.stack([key_offsets[at : at + SPAN] for at in range(0, PAIR, TILE)])
    half_dim = HEAD_SIZE // 2
    frequency = ROPE_BASE ** (-(jnp.arange(half_dim, dtype=jnp.float32) * 2.0) / HEAD_SIZE)
    angles = query_offsets.astype(jnp.float32)[:, None] * frequency[None, :]
    cosine, sine = jnp.cos(angles), jnp.sin(angles)
    cosine = jnp.concatenate([cosine, cosine], axis=1)
    sine = jnp.concatenate([-sine, sine], axis=1)
    query_offsets = query_offsets[:, None]

    rows = input_norm(moving, gain_in)
    from_low, from_high = shift_x(rows, 1), shift_x(rows, -1)
    part_out = lax.all_gather(part_out, "ctx", axis=0, tiled=True, axis_index_groups=ROWS)
    from_low, from_high, part_out, cosine, sine, query_offsets, key_offsets = together(
        from_low, from_high, part_out, cosine, sine, query_offsets, key_offsets
    )
    half = rows.shape[0] // 2
    far_low = shift_x(from_low[:half], 1)
    far_high = shift_x(from_high[half:], -1)
    own_rows = place_rows(place, [rows, from_high, far_low, far_high, from_low])
    other_rows = swap_cores(own_rows)

    tables = [gain_query.reshape(1, HEAD_SIZE), gain_key.reshape(1, HEAD_SIZE), cosine, sine]

    weights, part_out = together(weights, part_out)
    own_out = lax.all_gather(part_out, "ctx", axis=0, tiled=True, axis_index_groups=COLUMNS)
    q_own, kv_own = project(True, place, own_rows, weights, tables, "project_own")
    prev_own = next_pair(kv_own)
    q_other, kv_other = project(False, place, other_rows, weights, tables, "project_other")
    prev_other = next_pair(kv_other)
    blocks = [kv_own, kv_other, prev_own, prev_other]
    keep, give = attend(place, [q_own, q_other], blocks, query_offsets, key_offsets)
    other = swap_cores(give)
    both = jnp.stack([keep, other])
    attended = [both, shift_x(both, -1), shift_x(both, 2), shift_x(both, 1)]
    own_out, *attended[1:] = together(own_out, *attended[1:])
    other_out = swap_cores(own_out)
    sums = out_project(place, attended, own_out, other_out)
    sums = [sums[0], shift_x(sums[3], -1), shift_x(sums[2], 2), shift_x(sums[1], 1)]
    return final_norm(place, sums, tokens, gain_post)


def solution(mesh):
    in_specs = (
        P(("ctx", "tp"), None),
        P(),
        P("ctx", "tp"),
        P("ctx", "tp"),
        P("ctx", "tp"),
        P("tp", "ctx"),
        P(),
        P(),
        P(),
        P(),
    )
    out_specs = P(("ctx", "tp"), None)
    return jax.shard_map(shards, mesh=mesh, in_specs=in_specs, out_specs=out_specs, check_vma=False)
```

```python
import functools

import jax
import jax.numpy as jnp
from jax import lax
from jax.experimental import pallas as pl
from jax.experimental.pallas import tpu as pltpu
from jax.sharding import PartitionSpec as P

HEAD_SIZE = 128
QS = 168
LOOKBACK_WINDOW = 1024
EPSILON = 1e-06
ROPE_BASE = 10000.0
Z, Y, C, X = 8, 4, 2, 4
BLOCK = 512
PAIR = 1024
VMEM = pltpu.VMEM
MIB = 1024 * 1024


def ctx_pairs(move):
    pairs = []
    for source in range(Z * Y * C):
        target = move(source // (Y * C), source // C % Y, source % C)
        if target is not None:
            z, y, c = target
            pairs.append((source, (z % Z) * Y * C + (y % Y) * C + c))
    return pairs


def swap_cores(value):
    return lax.ppermute(value, "ctx", ctx_pairs(lambda z, y, c: (z, y, 1 - c)))


def shift_x(value, steps):
    return lax.ppermute(value, "tp", [(x, (x + steps) % X) for x in range(X)])


def next_pair(value):
    pairs = [(source, source + C) for source in range(Z * Y * C - C)]
    return lax.ppermute(value, "ctx", pairs)


def shift_y(value, steps):
    return lax.ppermute(value, "ctx", ctx_pairs(lambda z, y, c: (z, y + steps, c)))


def shift_z(value, steps):
    return lax.ppermute(value, "ctx", ctx_pairs(lambda z, y, c: (z + steps, y, c)))


def trade_x_z(value):
    pairs = []
    for source in range(Z * Y * C * X):
        ctx, x = source // X, source % X
        z, rest = ctx // (Y * C), ctx % (Y * C)
        pairs.append((source, ((x * 2 + z % 2) * Y * C + rest) * X + z // 2))
    return lax.ppermute(value, ("ctx", "tp"), pairs)


def together(*values):
    return lax.optimization_barrier(values)


ROWS = [[z * Y * C + y * C + c for y in range(Y)] for z in range(Z) for c in range(C)]
COLUMNS = [[z * Y * C + y * C + c for z in range(Z)] for y in range(Y) for c in range(C)]


def norm_body(rows_ref, gain_ref, out_ref):
    rows = rows_ref[...].astype(jnp.float32)
    scale = lax.rsqrt(jnp.mean(rows * rows, axis=-1, keepdims=True) + EPSILON)
    out_ref[...] = (rows * scale * gain_ref[...]).astype(jnp.bfloat16)


def input_norm(rows, gain):
    count, width = rows.shape
    step = 32
    return pl.pallas_call(
        norm_body,
        grid=(count // step,),
        in_specs=[
            pl.BlockSpec((step, width), lambda i: (i, 0)),
            pl.BlockSpec((1, width), lambda i: (0, 0)),
        ],
        out_specs=pl.BlockSpec((step, width), lambda i: (i, 0)),
        out_shape=jax.ShapeDtypeStruct(rows.shape, jnp.bfloat16),
        name="input_norm",
    )(rows, gain.reshape(1, width))


def head_norm_rope(raw, gain, cosine, sine):
    scale = lax.rsqrt(jnp.mean(raw * raw, axis=-1, keepdims=True) + EPSILON)
    normed = raw * scale * gain
    return normed * cosine + pltpu.roll(normed, HEAD_SIZE // 2, 1) * sine


PARTS = 3


def project_body(
    mine, place_ref, rows_hbm, weight_ref, gq_ref, gk_ref, cos_ref, sin_ref,
    q_ref, kv_ref, rows_ref, total_ref, sems,
):
    c = place_ref[3]
    start = pl.multiple_of((c if mine else 1 - c) * BLOCK, BLOCK)
    step = rows_ref.shape[1] // PARTS
    copies = []
    for k in range(PARTS):
        span = pl.ds(k * step, step)
        copies.append(
            pltpu.make_async_copy(rows_hbm.at[:, span], rows_ref.at[:, span], sems.at[k])
        )
    for copy in copies:
        copy.start()
    for k, copy in enumerate(copies):
        copy.wait()
        span = slice(k * step, (k + 1) * step)
        part = jnp.dot(
            rows_ref[:, span], weight_ref[span, :], preferred_element_type=jnp.float32
        )
        if k == 0:
            total_ref[...] = part
        else:
            total_ref[...] += part
    cosine, sine = cos_ref[pl.ds(start, BLOCK), :], sin_ref[pl.ds(start, BLOCK), :]
    heads = [total_ref[:, h * HEAD_SIZE : (h + 1) * HEAD_SIZE] for h in range(4)]
    kv_ref[0] = head_norm_rope(heads[2], gk_ref[...], cosine, sine).astype(jnp.bfloat16)
    kv_ref[1] = heads[3].astype(jnp.bfloat16)
    for h in range(2):
        q_ref[h] = head_norm_rope(heads[h], gq_ref[...], cosine, sine).astype(jnp.bfloat16)


def whole(shape):
    return pl.BlockSpec(shape, lambda i, p: (0,) * len(shape))


SMEM = pl.BlockSpec(memory_space=pltpu.SMEM)
HBM = pl.BlockSpec(memory_space=pltpu.HBM)
HELD = pl.BlockSpec(memory_space=pltpu.VMEM)


def project(mine, place, rows, weights, tables, name):
    width = weights.shape[0]
    head = jax.ShapeDtypeStruct((2, BLOCK, HEAD_SIZE), jnp.bfloat16)
    return pl.pallas_call(
        functools.partial(project_body, mine),
        in_specs=[SMEM, HBM] + [HELD] * 5,
        out_specs=[HELD] * 2,
        out_shape=[head] * 2,
        scratch_shapes=[
            pltpu.VMEM((BLOCK, width), jnp.bfloat16),
            pltpu.VMEM((BLOCK, 512), jnp.float32),
            pltpu.SemaphoreType.DMA((PARTS,)),
        ],
        compiler_params=pltpu.CompilerParams(vmem_limit_bytes=50 * MIB),
        cost_estimate=pl.CostEstimate(
            flops=2 * BLOCK * width * 512, bytes_accessed=12 * MIB, transcendentals=0
        ),
        name=name,
    )(place, rows, weights, *tables)


def rows_body(place_ref, *refs):
    pieces, out_ref = refs[:5], refs[5]
    x = place_ref[0]
    quarter, half = BLOCK // X, BLOCK // X // 2
    plan = [(0, 0, quarter), (1, 0, quarter), (2, 0, half), (2, half, half), (3, 0, quarter)]
    for piece, (rel, shift, size) in zip(pieces, plan):
        at = pl.multiple_of(lax.rem(x + rel, X) * quarter + shift, half)
        out_ref[pl.ds(at, size), :] = piece[...]


def place_rows(place, pieces):
    width = pieces[0].shape[1]
    step = 768
    return pl.pallas_call(
        rows_body,
        grid_spec=pltpu.PrefetchScalarGridSpec(
            num_scalar_prefetch=1,
            grid=(width // step,),
            in_specs=[pl.BlockSpec((p.shape[0], step), lambda i, p: (0, i)) for p in pieces],
            out_specs=pl.BlockSpec((BLOCK, step), lambda i, p: (0, i)),
        ),
        out_shape=jax.ShapeDtypeStruct((BLOCK, width), jnp.bfloat16),
        cost_estimate=pl.CostEstimate(flops=0, bytes_accessed=11 * MIB, transcendentals=0),
        name="place_rows",
    )(place, *pieces)


TILE = 128
SPAN = PAIR + TILE


def attend_body(
    place_ref, qmine_ref, qother_ref, mine_ref, other_ref, pmine_ref, pother_ref,
    qoff_ref, koff_ref, keep_ref, give_ref, keys_ref, values_ref,
):
    c = place_ref[3]
    for base, refs in ((0, (pmine_ref, pother_ref)), (PAIR, (mine_ref, other_ref))):
        for block, ref in ((c, refs[0]), (1 - c, refs[1])):
            at = pl.multiple_of(base + block * BLOCK, BLOCK)
            keys_ref[pl.ds(at, BLOCK), :] = ref[0]
            values_ref[pl.ds(at, BLOCK), :] = ref[1]
    for block, q_ref, out_ref in ((1 - c, qother_ref, give_ref), (c, qmine_ref, keep_ref)):
        for tile in range(BLOCK // TILE):
            first, last = tile * TILE, (tile + 1) * TILE
            at = pl.multiple_of(block * BLOCK + first, TILE)
            keys = keys_ref[pl.ds(at, SPAN), :]
            values = values_ref[pl.ds(at, SPAN), :]
            gap = (
                qoff_ref[pl.ds(at, TILE), :]
                - koff_ref[pl.ds(block * (BLOCK // TILE) + tile, 1), :]
            )
            allowed = (gap >= 0) & (gap < LOOKBACK_WINDOW)
            for h in range(2):
                scores = lax.dot_general(
                    q_ref[h, first:last],
                    keys,
                    (((1,), (1,)), ((), ())),
                    preferred_element_type=jnp.float32,
                ) * QS ** (-0.5)
                scores = jnp.where(allowed, scores, -1e30)
                row_max = jnp.max(scores, axis=-1, keepdims=True)
                weights = jnp.exp(scores - row_max)
                totals = jnp.sum(weights, axis=-1, keepdims=True)
                mixed = jnp.dot(
                    weights.astype(jnp.bfloat16), values, preferred_element_type=jnp.float32
                )
                out_ref[first:last, h * HEAD_SIZE : (h + 1) * HEAD_SIZE] = (
                    mixed / totals
                ).astype(jnp.bfloat16)


def attend(place, queries, blocks, query_offsets, key_offsets):
    out = jax.ShapeDtypeStruct((BLOCK, 2 * HEAD_SIZE), jnp.bfloat16)
    return pl.pallas_call(
        attend_body,
        in_specs=[SMEM] + [HELD] * 8,
        out_specs=[HELD] * 2,
        out_shape=[out] * 2,
        scratch_shapes=[pltpu.VMEM((2 * PAIR, HEAD_SIZE), jnp.bfloat16)] * 2,
        compiler_params=pltpu.CompilerParams(vmem_limit_bytes=32 * MIB),
        cost_estimate=pl.CostEstimate(
            flops=4 * PAIR * SPAN * 256, bytes_accessed=3 * MIB, transcendentals=2 * PAIR * SPAN
        ),
        name="attend",
    )(place, *queries, *blocks, query_offsets, key_offsets)


def out_body(place_ref, *refs):
    pieces, (own_ref, other_ref, *outs) = refs[:X], refs[X:]
    rows_ref = outs[X]
    x = place_ref[0]
    quarter = BLOCK // X
    count = own_ref.shape[0] // X
    weights = jnp.concatenate(
        [
            ref[pl.ds(pl.multiple_of(lax.rem(x + k, X) * count, 16), count), :]
            for k in range(X)
            for ref in (own_ref, other_ref)
        ],
        axis=1,
    )
    for k, piece in enumerate(pieces):
        for side in range(2):
            slot = (2 * k + side) * 256
            for rel in range(X):
                at = pl.multiple_of(lax.rem(x + rel, X) * quarter, quarter)
                rows_ref[rel * quarter : (rel + 1) * quarter, slot : slot + 256] = piece[
                    side, pl.ds(at, quarter), :
                ]
    total = lax.dot_general(
        rows_ref[...], weights, (((1,), (1,)), ((), ())), preferred_element_type=jnp.float32
    )
    for rel, out_ref in enumerate(outs[:X]):
        out_ref[...] = total[rel * quarter : (rel + 1) * quarter].astype(jnp.bfloat16)


def out_project(place, pieces, own, other):
    count = own.shape[0] // X
    chunk = jax.ShapeDtypeStruct((BLOCK // X, count), jnp.bfloat16)
    return pl.pallas_call(
        out_body,
        in_specs=[SMEM] + [HELD] * (X + 2),
        out_specs=[HELD] * X,
        out_shape=[chunk] * X,
        scratch_shapes=[
            pltpu.VMEM((BLOCK, 2048), jnp.bfloat16),
        ],
        compiler_params=pltpu.CompilerParams(vmem_limit_bytes=28 * MIB),
        cost_estimate=pl.CostEstimate(
            flops=2 * BLOCK * count * 2048, bytes_accessed=9 * MIB, transcendentals=0
        ),
        name="out_project",
    )(place, *pieces, own, other)


def final_body(place_ref, *refs):
    pieces, (rows_ref, gain_ref, out_ref, stage_ref) = refs[:X], refs[X:]
    x = place_ref[0]
    for k, piece in enumerate(pieces):
        stage_ref[lax.rem(x + k, X)] = piece[...]
    step = 32
    for at in range(0, rows_ref.shape[0], step):
        summed = jnp.concatenate(
            [stage_ref[k, at : at + step].astype(jnp.float32) for k in range(X)], axis=1
        )
        scale = lax.rsqrt(jnp.mean(summed * summed, axis=-1, keepdims=True) + EPSILON)
        out = rows_ref[at : at + step].astype(jnp.float32) + summed * scale * gain_ref[...]
        out_ref[at : at + step] = out.astype(jnp.bfloat16)


def final_norm(place, pieces, rows, gain):
    width = rows.shape[1]
    return pl.pallas_call(
        final_body,
        in_specs=[SMEM] + [HELD] * (X + 2),
        out_specs=HELD,
        out_shape=jax.ShapeDtypeStruct(rows.shape, jnp.bfloat16),
        scratch_shapes=[pltpu.VMEM((X, rows.shape[0], width // X), jnp.bfloat16)],
        compiler_params=pltpu.CompilerParams(vmem_limit_bytes=32 * MIB),
        name="final_norm",
    )(place, *pieces, rows, gain.reshape(1, width))


def core_order(first, second, c):
    low = jnp.where(c == 0, first, second)
    high = jnp.where(c == 0, second, first)
    return low, high


def shards(
    tokens,
    positions,
    w_query,
    key_matrix,
    value_matrix,
    w_out,
    gain_in,
    gain_query,
    gain_key,
    gain_post,
):
    ctx = lax.axis_index("ctx")
    c, y, z, pair = ctx % C, ctx // C % Y, ctx // (Y * C), ctx // C
    x = lax.axis_index("tp")
    place = jnp.stack([x, y, z, c]).astype(jnp.int32)
    width = tokens.shape[1]

    out_rows = w_out.T
    sides = [
        jnp.concatenate(
            [
                w_query[:, side * 256 : side * 256 + 256],
                key_matrix[:, side * 128 : side * 128 + 128],
                value_matrix[:, side * 128 : side * 128 + 128],
                out_rows[:, side * 256 : side * 256 + 256],
            ],
            axis=1,
        )
        for side in range(2)
    ]
    mine, theirs = core_order(sides[0], sides[1], c)
    received = swap_cores(theirs)
    stacked = jnp.concatenate(core_order(mine, received, c), axis=0)
    part, part_out = stacked[:, :512], trade_x_z(stacked[:, 512:])
    part = lax.all_gather(part, "ctx", axis=0, tiled=True, axis_index_groups=ROWS)
    part, moving = together(part, tokens)
    weights = lax.all_gather(part, "ctx", axis=0, tiled=True, axis_index_groups=COLUMNS)

    start = pair * PAIR
    query_offsets = lax.dynamic_slice_in_dim(positions, start, PAIR, 0) - positions[0]
    before = lax.dynamic_slice_in_dim(positions, jnp.maximum(start - PAIR, 0), PAIR, 0)
    before = jnp.where(pair == 0, -(2**30), before - positions[0])
    key_offsets = jnp.concatenate([before, query_offsets])
    key_offsets = jnp.stack([key_offsets[at : at + SPAN] for at in range(0, PAIR, TILE)])
    half_dim = HEAD_SIZE // 2
    frequency = ROPE_BASE ** (-(jnp.arange(half_dim, dtype=jnp.float32) * 2.0) / HEAD_SIZE)
    angles = query_offsets.astype(jnp.float32)[:, None] * frequency[None, :]
    cosine, sine = jnp.cos(angles), jnp.sin(angles)
    cosine = jnp.concatenate([cosine, cosine], axis=1)
    sine = jnp.concatenate([-sine, sine], axis=1)
    query_offsets = query_offsets[:, None]

    rows = input_norm(moving, gain_in)
    from_low, from_high = shift_x(rows, 1), shift_x(rows, -1)
    part_out = lax.all_gather(part_out, "ctx", axis=0, tiled=True, axis_index_groups=ROWS)
    from_low, from_high, part_out, cosine, sine, query_offsets, key_offsets = together(
        from_low, from_high, part_out, cosine, sine, query_offsets, key_offsets
    )
    half = rows.shape[0] // 2
    far_low = shift_x(from_low[:half], 1)
    far_high = shift_x(from_high[half:], -1)
    own_rows = place_rows(place, [rows, from_high, far_low, far_high, from_low])
    other_rows = swap_cores(own_rows)

    tables = [gain_query.reshape(1, HEAD_SIZE), gain_key.reshape(1, HEAD_SIZE), cosine, sine]

    weights, part_out = together(weights, part_out)
    own_out = lax.all_gather(part_out, "ctx", axis=0, tiled=True, axis_index_groups=COLUMNS)
    q_own, kv_own = project(True, place, own_rows, weights, tables, "project_own")
    prev_own = next_pair(kv_own)
    q_other, kv_other = project(False, place, other_rows, weights, tables, "project_other")
    prev_other = next_pair(kv_other)
    blocks = [kv_own, kv_other, prev_own, prev_other]
    keep, give = attend(place, [q_own, q_other], blocks, query_offsets, key_offsets)
    other = swap_cores(give)
    both = jnp.stack([keep, other])
    attended = [both, shift_x(both, -1), shift_x(both, 2), shift_x(both, 1)]
    own_out, *attended[1:] = together(own_out, *attended[1:])
    other_out = swap_cores(own_out)
    sums = out_project(place, attended, own_out, other_out)
    sums = [sums[0], shift_x(sums[3], -1), shift_x(sums[2], 2), shift_x(sums[1], 1)]
    return final_norm(place, sums, tokens, gain_post)


def solution(mesh):
    in_specs = (
        P(("ctx", "tp"), None),
        P(),
        P("ctx", "tp"),
        P("ctx", "tp"),
        P("ctx", "tp"),
        P("tp", "ctx"),
        P(),
        P(),
        P(),
        P(),
    )
    out_specs = P(("ctx", "tp"), None)
    return jax.shard_map(shards, mesh=mesh, in_specs=in_specs, out_specs=out_specs, check_vma=False)
```
